32 devices in a mesh: dp: 16 (over z, x, core), tensor: 2 (over y).
Axes of the slice: x: 2, y: 2, z: 4, core: 2. Of those that a mesh axis runs over, the one named last changes fastest.
Arguments:
- features: bfloat16 [8192, 1280], P('dp'), may hold values from -6 to 6
- class_bias: float32 [1536], P('tensor')
- logits: bfloat16 [8192, 1536], P('dp', 'tensor'), may hold values from -12 to 12
- tile_lists: int32 [256, 2], P('dp'), may hold values from 0 to 15, all different within a row; in each aligned block of 16 rows (0 to 15, 16 to 31, ...) at most 4 rows name the same one
- valid_counts: int32 [16], P('dp'), may hold values from 192 to 512, as said below
Outputs:
- log_labels: float32 [8192, 1536], P('dp', 'tensor')
The draws below stay inside these ranges and needn't reach their ends.
Inputs may be any that keep to these rules, and one draw needn't show every extreme that they name: `tile_lists`: each row names 2 different tiles; among the 16 rows of one index of dp no tile is named more than 4 times. `valid_counts`: some tile is fully valid.
All inputs are finite; a program needn't handle non-finite values.
Results may differ from the reference program's by a relative error of at most 0.0005.
Values may be sent and summed in bfloat16 or wider, within the bound.
A program may use at most 128 MiB of HBM per device.

```python
import math
import jax
import jax.numpy as jnp
import numpy as np
from jax import lax

D = 1280
TILE = 512
QB = 32
NT = 2
SWEEPS = 2
NBLK = 16
CAP = 4
TILES = 16
ROWS = 8192
BLOCKS = 256
CLS = 1536


def draw_class_bias(key, part):
    index = jnp.arange(CLS, dtype=jnp.float32)
    noise = jnp.clip(jax.random.normal(key, (CLS,), jnp.float32), -2.5, 2.5)
    return 1.2 * index / CLS + 0.5 * noise


def draw_valid_counts(key, part):
    first_key = jax.random.fold_in(key, 11)
    second_key = jax.random.fold_in(key, 23)
    member_counts = jax.random.randint(first_key, (TILES,), 3 * TILE // 8, TILE + 1)
    where_full = jax.random.randint(second_key, (), 0, TILES)
    return member_counts.at[where_full].set(TILE)


def levels(key, dims, cuts, least, top_value):
    gain = 1.0
    for position, shards_of in cuts:
        heights = jax.random.uniform(jax.random.fold_in(jax.random.fold_in(key, 6), position), (shards_of,), jnp.float32, least / len(cuts), top_value / len(cuts))
        gain = gain * jnp.repeat(jnp.exp(heights), dims[position] // shards_of).reshape((-1,) + (1,) * (len(dims) - 1 - position))
    return gain


def deal_out(key, own, number, rows, count, top, bound, slope):
    sequence = jax.random.permutation(key, count)
    packed, ordinary = load_shares(count, rows * top, bound, slope, True), load_shares(count, rows * top, bound, slope, False)
    places = jnp.arange(count)

    def named(sizes, offset_by):
        used = int((sizes > 0).sum())
        fixed = max(1, used // 4)
        moved = fixed + (places - fixed + offset_by * (used - fixed)) % max(1, count - fixed)
        return jnp.zeros((count,), jnp.int32).at[sequence[jnp.where(places < fixed, places, moved)]].set(jnp.asarray(sizes, jnp.int32))

    sizes = jnp.where(number % 4 == 0, named(packed, number // 4), named(ordinary, number - number // 4 - 1))
    mixed = jax.random.permutation(jax.random.fold_in(own, 3), count)
    source_of, taker = mixed[0:count // 2 * 2:2], mixed[1:count // 2 * 2:2]
    room = jnp.minimum(sizes[source_of] - 1, bound - sizes[taker]) // 2
    room = jnp.where((source_of == sequence[0]) | (taker == sequence[0]) | (sizes[taker] == 0), 0, jnp.maximum(room, 0))
    moved = jax.random.randint(jax.random.fold_in(own, 4), (count // 2,), 0, 1 << 20) % (room + 1)
    sizes = sizes.at[source_of].add(-moved).at[taker].add(moved)
    items = jnp.searchsorted(jnp.cumsum(sizes), jnp.arange(rows * top), side="right").astype(jnp.int32)
    listing = items.reshape(top, rows).T
    listing = listing[jax.random.permutation(jax.random.fold_in(own, 1), rows)]
    offset_by = jax.random.randint(jax.random.fold_in(own, 2), (rows, 1), 0, top)
    return jnp.take_along_axis(listing, (jnp.arange(top)[None, :] + offset_by) % top, axis=1)


def load_shares(amount, total, limit, lean, full):
    portions = [(1 << 20) // math.isqrt(rank ** lean) + 1 for rank in range(1, amount + 1)]
    largest = limit if full else min(limit, max(-(-total // amount), total * portions[0] // sum(portions)))
    least = 1 if total - largest >= amount - 1 else 0
    given, rest = [largest] + [least] * (amount - 1), total - largest - least * (amount - 1)
    while rest > 0:
        movable = [i for i in range(1, amount) if given[i] < largest] or [i for i in range(1, amount) if given[i] < limit]
        whole, budget = sum([portions[i] for i in movable]), rest
        for i in movable:
            more = min(limit - given[i], max(1, budget * portions[i] // whole), rest)
            given[i] = given[i] + more
            rest = rest - more
    return np.array(given)


def centred(stream_key, shape, scale, bound, pieces=(), held_as=jnp.bfloat16):
    drawn = jax.random.normal(stream_key, shape, jnp.float32) * scale
    if len(pieces) > 0:
        drawn = levels(stream_key, shape, pieces, -0.22, 0.18) * drawn
    return jnp.clip(drawn, min=-bound, max=bound).astype(held_as)


def setup_inputs(seed: int = 0) -> dict:
    keys = jax.random.split(jax.random.key(seed), 6)
    features = centred(keys[0], (ROWS, D), 1.0, 6.0, ((0, 16),))
    class_bias = draw_class_bias(jax.random.fold_in(keys[5], 71), 0)
    logits = centred(keys[2], (ROWS, CLS), 3.0, 12.0, ((0, 16), (1, 2)))
    tile_lists_keys = jax.random.split(jax.random.fold_in(keys[3], 1), BLOCKS // NBLK)
    tile_lists_turns = jax.random.permutation(jax.random.fold_in(keys[3], 3), BLOCKS // NBLK)
    tile_lists = jax.vmap(lambda own, number: deal_out(jax.random.fold_in(keys[3], 2), own, number, NBLK, TILES, NT, CAP, 2))(tile_lists_keys, tile_lists_turns).reshape((BLOCKS, NT))
    valid_counts = draw_valid_counts(jax.random.fold_in(keys[5], 71), 0)
    return dict(features=features, class_bias=class_bias, logits=logits, tile_lists=tile_lists, valid_counts=valid_counts)


ALPHA = 0.75
SOFTMAX_TEMPER = 0.05
EPSILON = 1e-06

def unitnorm_rows(features):
    wide = features.astype(jnp.float32)
    scale = lax.rsqrt(lax.optimization_barrier(jnp.mean(wide * wide, axis=1, keepdims=True)) + EPSILON)
    return (wide * scale / math.sqrt(wide.shape[1])).astype(jnp.bfloat16)

def reference(features, class_bias, logits, tile_lists, valid_counts):
    adjusted = logits.astype(jnp.float32) + class_bias[None, :]
    exponentials = jnp.exp(adjusted)
    prior = (exponentials / lax.optimization_barrier(jnp.sum(exponentials, axis=1))[:, None]).astype(jnp.bfloat16)
    normalized = unitnorm_rows(features)
    query_blocks = normalized.reshape(BLOCKS, QB, D)
    columns = jnp.arange(TILE, dtype=jnp.int32)

    def block_weights(inputs):
        query_vectors, tile_ids = inputs

        def one_tile(tile_number):
            tile_row_block = lax.dynamic_slice_in_dim(normalized, (tile_number * TILE).astype(jnp.int32), TILE, 0)
            affinity_scores = jnp.dot(query_vectors, tile_row_block.T, preferred_element_type=jnp.float32) / SOFTMAX_TEMPER
            return jnp.where(columns[None, :] < valid_counts[tile_number], jnp.exp(affinity_scores), 0.0).astype(jnp.bfloat16)
        return jax.vmap(one_tile)(tile_ids)
    weights = lax.map(block_weights, (query_blocks, tile_lists))
    denominator = lax.optimization_barrier(jnp.sum(lax.optimization_barrier(jnp.sum(weights.astype(jnp.float32), axis=3)), axis=1)).reshape(ROWS)
    prior_float = prior.astype(jnp.float32)
    label_matrix = prior
    spread = prior_float
    for sweep_index in range(SWEEPS):
        current = label_matrix

        def block_numerator(inputs):
            block_weight, tile_ids = inputs

            def one_tile(tile_weight, tile_number):
                tile_row_block = lax.dynamic_slice_in_dim(current, (tile_number * TILE).astype(jnp.int32), TILE, 0)
                partial_sum = jnp.dot(tile_weight, tile_row_block, preferred_element_type=jnp.float32).astype(jnp.bfloat16)
                return lax.optimization_barrier(partial_sum).astype(jnp.float32)
            return lax.optimization_barrier(jnp.sum(jax.vmap(one_tile)(block_weight, tile_ids), axis=0))
        numerator = lax.map(block_numerator, (weights, tile_lists)).reshape(ROWS, CLS)
        spread = ALPHA * numerator / denominator[:, None] + (1.0 - ALPHA) * prior_float
        label_matrix = spread.astype(jnp.bfloat16)
    return jnp.log(spread)
```

```python
import functools
import math

import jax
import jax.numpy as jnp
from jax import lax
from jax.experimental import pallas as pl
from jax.experimental.pallas import tpu as pltpu
from jax.sharding import PartitionSpec as P

ALPHA = 0.75
SOFTMAX_TEMPER = 0.05
EPSILON = 1e-06
GROUP = 8
SPLITS = 2
VMEM_BYTES = 60 * 1024 * 1024


def unitnorm_rows(features):
    wide = features.astype(jnp.float32)
    scale = lax.rsqrt(jnp.mean(wide * wide, axis=1, keepdims=True) + EPSILON)
    return (wide * scale / math.sqrt(wide.shape[1])).astype(jnp.bfloat16)


def weights_kernel(
    block_rows, tile_rows, step_tile, slot_block, slot_first, used, counts, memory, out, factor,
    held, total, sem
):
    step = pl.program_id(0)
    rows = memory.shape[0]

    @pl.when(step == 0)
    def _():
        copy = pltpu.make_async_copy(memory, held.at[pl.ds(0, rows)], sem)
        copy.start()
        copy.wait()

    @pl.when(step < used[0])
    def _():
        tile = step_tile[step]
        starts = [
            pl.multiple_of(slot_block[step * GROUP + j] * block_rows, block_rows)
            for j in range(GROUP)
        ]
        queries = jnp.concatenate([held[pl.ds(s, block_rows), :] for s in starts], axis=0)
        keys = held[pl.ds(pl.multiple_of(tile * tile_rows, tile_rows), tile_rows), :]
        scores = lax.dot_general(
            queries, keys, (((1,), (1,)), ((), ())), preferred_element_type=jnp.float32
        )
        columns = lax.broadcasted_iota(jnp.int32, scores.shape, 1)
        weights = jnp.where(
            columns < counts[tile], jnp.exp(scores * (1.0 / SOFTMAX_TEMPER)), 0.0
        ).astype(jnp.bfloat16)
        out[...] = weights
        sums = jnp.sum(weights.astype(jnp.float32), axis=1, keepdims=True)
        sums = jnp.broadcast_to(sums, (sums.shape[0], 128))
        for j in range(GROUP):
            where = pl.ds(starts[j], block_rows)
            old = jnp.where(slot_first[step * GROUP + j] == 1, 0.0, total[where, :])
            total[where, :] = old + sums[j * block_rows : (j + 1) * block_rows]

    @pl.when(step == pl.num_programs(0) - 1)
    def _():
        factor[...] = ALPHA / total[pl.ds(0, rows), :]


def labels_kernel(
    chunks, block_rows, own_slots, step_tile, slot_block, slot_first, used, own_block, own_first,
    me, weights, own_weights, prior, factor, own_prior, own_factor, out, total, own_total
):
    step = pl.program_id(0)
    tile_rows = prior.shape[0]

    def add(into, part, blocks, firsts, base, number):
        part = part.astype(jnp.bfloat16).astype(jnp.float32)
        for j in range(number):
            start = pl.multiple_of(blocks[base + j] * block_rows, block_rows)
            where = pl.ds(start, block_rows)
            old = jnp.where(firsts[base + j] == 1, 0.0, into[where, :])
            into[where, :] = old + part[j * block_rows : (j + 1) * block_rows]

    @pl.when(step < used[0])
    def _():
        part = jnp.dot(weights[...], prior[...], preferred_element_type=jnp.float32)
        add(total, part, slot_block, slot_first, step * GROUP, GROUP)

    @pl.when(step >= chunks)
    def _():
        tile = step - chunks
        rows = pl.ds(pl.multiple_of(tile * tile_rows, tile_rows), tile_rows)
        labels = total[rows, :] * factor[:, :1] + (1.0 - ALPHA) * prior[...].astype(jnp.float32)
        part = jnp.dot(
            own_weights[...], labels.astype(jnp.bfloat16), preferred_element_type=jnp.float32
        )
        add(own_total, part, own_block, own_first, tile * own_slots, own_slots)

    @pl.when(step == pl.num_programs(0) - 1)
    def _():
        spread = own_total[pl.ds(0, tile_rows), :] * own_factor[:, :1]
        out[...] = jnp.log(spread + (1.0 - ALPHA) * own_prior[...].astype(jnp.float32))


def on_device(features, class_bias, logits, tile_lists, valid_counts):
    devices = lax.axis_size("dp")
    twins = lax.axis_size("tensor")
    own_rows, width = features.shape
    block_count, listed = tile_lists.shape
    block_rows = own_rows // block_count
    rows = own_rows * devices
    blocks = block_count * devices
    requests = blocks * listed
    chunks = (requests + devices * (GROUP - 1)) // GROUP
    slots = chunks * GROUP
    me = lax.axis_index("dp").astype(jnp.int32)
    twin = lax.axis_index("tensor")

    normalized = unitnorm_rows(features)
    share = own_rows // twins
    mine = lax.dynamic_slice_in_dim(normalized, twin * share, share, 0)
    memory = lax.all_gather(mine, ("dp", "tensor"), axis=0, tiled=True)

    adjusted = logits.astype(jnp.float32) + class_bias[None, :]
    exponentials = jnp.exp(adjusted)
    row_totals = lax.psum(jnp.sum(exponentials, axis=1), "tensor")
    prior = (exponentials / row_totals[:, None]).astype(jnp.bfloat16)
    part_width = prior.shape[1] // SPLITS
    own_priors = [prior[:, s * part_width : (s + 1) * part_width] for s in range(SPLITS)]
    priors = [lax.all_gather(p, "dp", axis=0, tiled=True) for p in own_priors]

    small = jnp.concatenate([tile_lists.reshape(-1), valid_counts])
    small = lax.all_gather(small, "dp", axis=0, tiled=False)
    counts = small[:, -1]
    owners = small[:, :-1].reshape(-1)
    pairs = owners.reshape(-1, listed)
    firsts = jnp.stack([pairs[:, 0] < pairs[:, 1], pairs[:, 1] < pairs[:, 0]], axis=1)
    firsts = firsts.reshape(-1).astype(jnp.int32)
    hits = (owners[:, None] == jnp.arange(devices, dtype=jnp.int32)[None, :]).astype(jnp.int32)
    running = jnp.cumsum(hits, axis=0)
    earlier = jnp.sum((running - hits) * hits, axis=1)
    tile_chunks = (running[-1] + GROUP - 1) // GROUP
    ends = jnp.cumsum(tile_chunks)
    bases = ends - tile_chunks
    position = jnp.sum(hits * bases[None, :], axis=1) * GROUP + earlier
    matches = position[None, :] == jnp.arange(slots, dtype=jnp.int32)[:, None]
    request_ids = jnp.arange(requests, dtype=jnp.int32)
    filled = jnp.any(matches, axis=1)
    source = jnp.sum(jnp.where(matches, request_ids[None, :], 0), axis=1)
    slot_block = jnp.where(filled, source // listed, blocks)
    slot_first = jnp.sum(jnp.where(matches, firsts[None, :], 0), axis=1)
    used = ends[-1:]
    steps = jnp.minimum(jnp.arange(chunks, dtype=jnp.int32), used[0] - 1)
    chunk_tile = jnp.sum((steps[:, None] >= ends[None, :]).astype(jnp.int32), axis=1)
    step_tile = jnp.concatenate([chunk_tile, jnp.arange(devices, dtype=jnp.int32)])

    capacity = max(2, 64 // devices)
    own_requests = block_count * listed
    own_owners = tile_lists.reshape(-1)
    own_hits = (own_owners[:, None] == jnp.arange(devices, dtype=jnp.int32)[None, :]).astype(
        jnp.int32
    )
    own_earlier = jnp.sum((jnp.cumsum(own_hits, axis=0) - own_hits) * own_hits, axis=1)
    own_place = own_owners * capacity + own_earlier
    own_matches = (
        own_place[None, :] == jnp.arange(devices * capacity, dtype=jnp.int32)[:, None]
    )
    own_filled = jnp.any(own_matches, axis=1)

    def placed(values):
        return jnp.sum(jnp.where(own_matches, values[None, :], 0), axis=1)

    own_first = placed(lax.dynamic_slice_in_dim(firsts, me * own_requests, own_requests))
    own_slot = placed(lax.dynamic_slice_in_dim(position, me * own_requests, own_requests))
    own_block = jnp.where(
        own_filled, placed(jnp.arange(own_requests, dtype=jnp.int32) // listed), block_count
    )

    def one_chunk(step, tiles, sb, sf, n, *rest):
        return (jnp.minimum(step, n[0] - 1), 0)

    weights, factor = pl.pallas_call(
        functools.partial(weights_kernel, block_rows, own_rows),
        grid_spec=pltpu.PrefetchScalarGridSpec(
            num_scalar_prefetch=5,
            grid=(chunks,),
            in_specs=[pl.BlockSpec(memory_space=pl.ANY)],
            out_specs=[
                pl.BlockSpec((GROUP * block_rows, own_rows), one_chunk),
                pl.BlockSpec((rows, 128), lambda *a: (0, 0), pipeline_mode=pl.Buffered(1)),
            ],
            scratch_shapes=[
                pltpu.VMEM((rows + block_rows, width), jnp.bfloat16),
                pltpu.VMEM((rows + block_rows, 128), jnp.float32),
                pltpu.SemaphoreType.DMA,
            ],
        ),
        out_shape=[
            jax.ShapeDtypeStruct((slots * block_rows, own_rows), jnp.bfloat16),
            jax.ShapeDtypeStruct((rows, 128), jnp.float32),
        ],
        compiler_params=pltpu.CompilerParams(vmem_limit_bytes=VMEM_BYTES),
        cost_estimate=pl.CostEstimate(
            flops=2 * requests * block_rows * own_rows * width,
            bytes_accessed=rows * width * 2 + slots * block_rows * own_rows * 2,
            transcendentals=requests * block_rows * own_rows,
        ),
        name="weights",
    )(step_tile, slot_block, slot_first, used, counts, memory)

    own_weights = weights.reshape(slots, block_rows, own_rows)[own_slot]
    own_weights = own_weights.reshape(devices * capacity * block_rows, own_rows)
    own_factor = lax.dynamic_slice_in_dim(factor, me * own_rows, own_rows, 0)

    def tile_of(step, tiles, *rest):
        return (tiles[step], 0)

    def late_tile(step, *rest):
        return (jnp.maximum(step - chunks, 0), 0)

    def same(*a):
        return (0, 0)

    outs = []
    for piece, own_piece in zip(priors, own_priors):
        outs.append(
            pl.pallas_call(
                functools.partial(labels_kernel, chunks, block_rows, capacity),
                grid_spec=pltpu.PrefetchScalarGridSpec(
                    num_scalar_prefetch=7,
                    grid=(chunks + devices,),
                    in_specs=[
                        pl.BlockSpec((GROUP * block_rows, own_rows), one_chunk),
                        pl.BlockSpec((capacity * block_rows, own_rows), late_tile),
                        pl.BlockSpec((own_rows, part_width), tile_of),
                        pl.BlockSpec((own_rows, 128), late_tile),
                        pl.BlockSpec((own_rows, part_width), same),
                        pl.BlockSpec((own_rows, 128), same),
                    ],
                    out_specs=pl.BlockSpec((own_rows, part_width), same),
                    scratch_shapes=[
                        pltpu.VMEM((rows + block_rows, part_width), jnp.float32),
                        pltpu.VMEM((own_rows + block_rows, part_width), jnp.float32),
                    ],
                ),
                out_shape=jax.ShapeDtypeStruct((own_rows, part_width), jnp.float32),
                compiler_params=pltpu.CompilerParams(vmem_limit_bytes=VMEM_BYTES),
                cost_estimate=pl.CostEstimate(
                    flops=2 * requests * block_rows * own_rows * part_width,
                    bytes_accessed=slots * block_rows * own_rows * 2,
                    transcendentals=0,
                ),
                name="labels",
            )(
                step_tile, slot_block, slot_first, used, own_block, own_first, me.reshape(1),
                weights, own_weights, piece, factor, own_piece, own_factor,
            )
        )
    return jnp.concatenate(outs, axis=1)


def solution(mesh):
    in_specs = (P("dp", None), P("tensor"), P("dp", "tensor"), P("dp", None), P("dp"))
    out_specs = P("dp", "tensor")
    return jax.shard_map(
        on_device, mesh=mesh, in_specs=in_specs, out_specs=out_specs, check_vma=False
    )
```

```python
import functools
import math

import jax
import jax.numpy as jnp
from jax import lax
from jax.experimental import pallas as pl
from jax.experimental.pallas import tpu as pltpu
from jax.sharding import PartitionSpec as P

ALPHA = 0.75
SOFTMAX_TEMPER = 0.05
EPSILON = 1e-06
GROUP = 16
VMEM_BYTES = 60 * 1024 * 1024


def unitnorm_rows(features):
    wide = features.astype(jnp.float32)
    scale = lax.rsqrt(jnp.mean(wide * wide, axis=1, keepdims=True) + EPSILON)
    return (wide * scale / math.sqrt(wide.shape[1])).astype(jnp.bfloat16)


def weights_kernel(
    block_rows, tile_rows, step_tile, slot_block, slot_first, used, counts, memory, out, factor,
    held, total, sem
):
    step = pl.program_id(0)
    rows = memory.shape[0]

    @pl.when(step == 0)
    def _():
        copy = pltpu.make_async_copy(memory, held.at[pl.ds(0, rows)], sem)
        copy.start()
        copy.wait()

    @pl.when(step < used[0])
    def _():
        tile = step_tile[step]
        starts = [
            pl.multiple_of(slot_block[step * GROUP + j] * block_rows, block_rows)
            for j in range(GROUP)
        ]
        queries = jnp.concatenate([held[pl.ds(s, block_rows), :] for s in starts], axis=0)
        keys = held[pl.ds(pl.multiple_of(tile * tile_rows, tile_rows), tile_rows), :]
        scores = lax.dot_general(
            queries, keys, (((1,), (1,)), ((), ())), preferred_element_type=jnp.float32
        )
        columns = lax.broadcasted_iota(jnp.int32, scores.shape, 1)
        weights = jnp.where(
            columns < counts[tile], jnp.exp(scores * (1.0 / SOFTMAX_TEMPER)), 0.0
        ).astype(jnp.bfloat16)
        out[...] = weights
        sums = jnp.sum(weights.astype(jnp.float32), axis=1, keepdims=True)
        sums = jnp.broadcast_to(sums, (sums.shape[0], 128))
        for j in range(GROUP):
            where = pl.ds(starts[j], block_rows)
            old = jnp.where(slot_first[step * GROUP + j] == 1, 0.0, total[where, :])
            total[where, :] = old + sums[j * block_rows : (j + 1) * block_rows]

    @pl.when(step == pl.num_programs(0) - 1)
    def _():
        factor[...] = ALPHA / total[pl.ds(0, rows), :]


def labels_kernel(
    chunks, block_rows, own_slots, step_tile, slot_block, slot_first, used, own_block, own_first,
    me, weights, own_weights, prior, factor, own_prior, own_factor, out, total, own_total
):
    step = pl.program_id(0)
    tile_rows = prior.shape[0]

    def add(into, part, blocks, firsts, base, number):
        part = part.astype(jnp.bfloat16).astype(jnp.float32)
        for j in range(number):
            start = pl.multiple_of(blocks[base + j] * block_rows, block_rows)
            where = pl.ds(start, block_rows)
            old = jnp.where(firsts[base + j] == 1, 0.0, into[where, :])
            into[where, :] = old + part[j * block_rows : (j + 1) * block_rows]

    @pl.when(step < used[0])
    def _():
        part = jnp.dot(weights[...], prior[...], preferred_element_type=jnp.float32)
        add(total, part, slot_block, slot_first, step * GROUP, GROUP)

    @pl.when(step >= chunks)
    def _():
        tile = step - chunks
        rows = pl.ds(pl.multiple_of(tile * tile_rows, tile_rows), tile_rows)
        labels = total[rows, :] * factor[:, :1] + (1.0 - ALPHA) * prior[...].astype(jnp.float32)
        part = jnp.dot(
            own_weights[...], labels.astype(jnp.bfloat16), preferred_element_type=jnp.float32
        )
        add(own_total, part, own_block, own_first, tile * own_slots, own_slots)

    @pl.when(step == pl.num_programs(0) - 1)
    def _():
        spread = own_total[pl.ds(0, tile_rows), :] * own_factor[:, :1]
        out[...] = jnp.log(spread + (1.0 - ALPHA) * own_prior[...].astype(jnp.float32))


def gather_kernel(features, labels, memory, priors, recv, send, local):
    dp, y = lax.axis_index("dp"), lax.axis_index("tensor")
    z, x, c = dp // 4, (dp // 2) % 2, dp % 2
    rows = features.shape[0]
    half = rows // 2

    def index(zz, xx):
        return zz * 4 + xx * 2 + c

    def region(t, kind):
        if kind == 2:
            return priors.at[pl.ds(pl.multiple_of(t * rows, rows), rows)]
        h = y if kind == 0 else 1 - y
        return memory.at[pl.ds(pl.multiple_of(t * rows + h * half, half), half)]

    def own_region(kind):
        if kind == 2:
            return labels
        h = y if kind == 0 else 1 - y
        return features.at[pl.ds(pl.multiple_of(h * half, half), half)]

    def partner(way):
        if way == 0:
            return {"dp": dp - 4}
        if way == 1:
            return {"dp": dp + 4}
        if way == 2:
            return {"dp": dp + 2 - 4 * x}
        if way == 3:
            return {"tensor": 1 - y}
        return {"dp": dp + 1 - 2 * c}

    def reach(way):
        if way == 0:
            return z > 0
        if way == 1:
            return z < 3
        return None

    def guarded(conditions, body):
        conditions = [q for q in conditions if q is not None]
        if not conditions:
            body()
        else:
            both = conditions[0]
            for q in conditions[1:]:
                both = jnp.logical_and(both, q)
            pl.when(both)(body)

    sent = []

    def copy(zz, xx, kind, way, own):
        t = index(zz, xx)
        arrives = 1 if way == 3 else kind
        return pltpu.make_async_remote_copy(
            src_ref=own_region(kind) if own else region(t, kind),
            dst_ref=region(t, kind),
            send_sem=send.at[zz * 2 + xx, kind, way],
            recv_sem=recv.at[t, arrives],
            device_id=partner(way),
            device_id_type=pl.DeviceIdType.MESH,
        )

    def push(zz, xx, kind, ways, exists=None, own=False):
        for way in ways:
            guards = (exists, reach(way))
            guarded(guards, lambda way=way: copy(zz, xx, kind, way, own).start())
            sent.append((guards, zz, xx, kind, way, own))

    def landed(t, kind):
        pltpu.make_async_remote_copy(
            src_ref=region(t, kind), dst_ref=region(t, kind),
            send_sem=send.at[0, 0, 0], recv_sem=recv.at[t, kind],
            device_id=partner(4), device_id_type=pl.DeviceIdType.MESH,
        ).wait_recv()

    def column(distance):
        if distance == 0:
            return [(z, None, (0, 1))]
        return [
            (z - distance, z >= distance, (1,)),
            (z + distance, z + distance < 4, (0,)),
        ]

    def near(distance, kind):
        for zz, exists, ways in column(distance):
            guarded((exists,), lambda zz=zz: landed(index(zz, x), kind))
            onward = ways + ((2, 3, 4) if kind == 0 else (2, 4))
            push(zz, x, kind, onward, exists)

    def across(distance, kind):
        for zz, exists, _ in column(distance):
            guarded((exists,), lambda zz=zz: landed(index(zz, 1 - x), kind))
            push(zz, 1 - x, kind, (3, 4) if kind == 0 else (4,), exists)

    def mirrored(distance, xx):
        for zz, exists, _ in column(distance):
            guarded((exists,), lambda zz=zz: landed(index(zz, xx), 1))
            push(zz, xx, 1, (4,), exists)

    barrier = pltpu.get_barrier_semaphore()
    for way in range(5):
        guarded(
            (reach(way),),
            lambda way=way: pl.semaphore_signal(
                barrier, inc=1, device_id=partner(way), device_id_type=pl.DeviceIdType.MESH
            ),
        )
    pl.semaphore_wait(barrier, 4 + z * (3 - z) // 2)

    push(z, x, 0, (0, 1, 2, 4), own=True)
    keep = pl.ds(pl.multiple_of(dp * rows, rows), rows)
    copies = [
        pltpu.make_async_copy(features, memory.at[keep], local.at[0]),
        pltpu.make_async_copy(labels, priors.at[keep], local.at[1]),
    ]
    for one in copies:
        one.start()
    for distance in (1, 2, 3):
        near(distance, 0)
        across(distance - 1, 0)
        if distance == 2:
            push(z, x, 2, (0, 1, 2, 4), own=True)
            push(z, x, 1, (4,), own=True)
    across(3, 0)
    for distance in (1, 2, 3):
        near(distance, 2)
        across(distance - 1, 2)
        mirrored(distance, x)
        mirrored(distance - 1, 1 - x)
    mirrored(3, 1 - x)
    across(3, 2)
    for zz in range(4):
        for xx in range(2):
            for kind in range(3):
                landed(zz * 4 + xx * 2 + 1 - c, kind)
    for guards, zz, xx, kind, way, own in sent:
        guarded(
            guards,
            lambda zz=zz, xx=xx, kind=kind, way=way, own=own: copy(
                zz, xx, kind, way, own
            ).wait_send(),
        )
    for one in copies:
        one.wait()


def gather_all(normalized, prior, devices):
    rows, width = normalized.shape
    classes = prior.shape[1]
    return pl.pallas_call(
        gather_kernel,
        in_specs=[pl.BlockSpec(memory_space=pl.ANY)] * 2,
        out_specs=[pl.BlockSpec(memory_space=pl.ANY)] * 2,
        out_shape=[
            jax.ShapeDtypeStruct((devices * rows, width), normalized.dtype),
            jax.ShapeDtypeStruct((devices * rows, classes), prior.dtype),
        ],
        scratch_shapes=[
            pltpu.SemaphoreType.DMA((devices, 3)),
            pltpu.SemaphoreType.DMA((8, 3, 5)),
            pltpu.SemaphoreType.DMA((2,)),
        ],
        compiler_params=pltpu.CompilerParams(collective_id=0, has_side_effects=True),
        cost_estimate=pl.CostEstimate(
            flops=0, bytes_accessed=2 * devices * rows * (width + classes) * 2, transcendentals=0
        ),
        name="gather",
    )(normalized, prior)


def on_device(features, class_bias, logits, tile_lists, valid_counts):
    devices = lax.axis_size("dp")
    twins = lax.axis_size("tensor")
    own_rows, width = features.shape
    block_count, listed = tile_lists.shape
    block_rows = own_rows // block_count
    rows = own_rows * devices
    blocks = block_count * devices
    requests = blocks * listed
    chunks = (requests + devices * (GROUP - 1)) // GROUP
    slots = chunks * GROUP
    me = lax.axis_index("dp").astype(jnp.int32)
    twin = lax.axis_index("tensor")

    normalized = unitnorm_rows(features)
    adjusted = logits.astype(jnp.float32) + class_bias[None, :]
    exponentials = jnp.exp(adjusted)
    row_totals = lax.psum(jnp.sum(exponentials, axis=1), "tensor")
    prior = (exponentials / row_totals[:, None]).astype(jnp.bfloat16)
    grid_links = devices == 16 and twins == 2
    splits = 1 if grid_links else 2
    part_width = prior.shape[1] // splits
    own_priors = [prior[:, s * part_width : (s + 1) * part_width] for s in range(splits)]
    if grid_links:
        memory, gathered = gather_all(normalized, prior, devices)
        priors = [gathered]
    else:
        share = own_rows // twins
        mine = lax.dynamic_slice_in_dim(normalized, twin * share, share, 0)
        memory = lax.all_gather(mine, ("dp", "tensor"), axis=0, tiled=True)
        priors = [lax.all_gather(p, "dp", axis=0, tiled=True) for p in own_priors]

    small = jnp.concatenate([tile_lists.reshape(-1), valid_counts])
    small = lax.all_gather(small, "dp", axis=0, tiled=False)
    counts = small[:, -1]
    owners = small[:, :-1].reshape(-1)
    pairs = owners.reshape(-1, listed)
    firsts = jnp.stack([pairs[:, 0] < pairs[:, 1], pairs[:, 1] < pairs[:, 0]], axis=1)
    firsts = firsts.reshape(-1).astype(jnp.int32)
    hits = (owners[:, None] == jnp.arange(devices, dtype=jnp.int32)[None, :]).astype(jnp.int32)
    running = jnp.cumsum(hits, axis=0)
    earlier = jnp.sum((running - hits) * hits, axis=1)
    tile_chunks = (running[-1] + GROUP - 1) // GROUP
    ends = jnp.cumsum(tile_chunks)
    bases = ends - tile_chunks
    position = jnp.sum(hits * bases[None, :], axis=1) * GROUP + earlier
    matches = position[None, :] == jnp.arange(slots, dtype=jnp.int32)[:, None]
    request_ids = jnp.arange(requests, dtype=jnp.int32)
    filled = jnp.any(matches, axis=1)
    source = jnp.sum(jnp.where(matches, request_ids[None, :], 0), axis=1)
    slot_block = jnp.where(filled, source // listed, blocks)
    slot_first = jnp.sum(jnp.where(matches, firsts[None, :], 0), axis=1)
    used = ends[-1:]
    steps = jnp.minimum(jnp.arange(chunks, dtype=jnp.int32), used[0] - 1)
    chunk_tile = jnp.sum((steps[:, None] >= ends[None, :]).astype(jnp.int32), axis=1)
    step_tile = jnp.concatenate([chunk_tile, jnp.arange(devices, dtype=jnp.int32)])

    capacity = max(2, 64 // devices)
    own_requests = block_count * listed
    own_owners = tile_lists.reshape(-1)
    own_hits = (own_owners[:, None] == jnp.arange(devices, dtype=jnp.int32)[None, :]).astype(
        jnp.int32
    )
    own_earlier = jnp.sum((jnp.cumsum(own_hits, axis=0) - own_hits) * own_hits, axis=1)
    own_place = own_owners * capacity + own_earlier
    own_matches = (
        own_place[None, :] == jnp.arange(devices * capacity, dtype=jnp.int32)[:, None]
    )
    own_filled = jnp.any(own_matches, axis=1)

    def placed(values):
        return jnp.sum(jnp.where(own_matches, values[None, :], 0), axis=1)

    own_first = placed(lax.dynamic_slice_in_dim(firsts, me * own_requests, own_requests))
    own_slot = placed(lax.dynamic_slice_in_dim(position, me * own_requests, own_requests))
    own_block = jnp.where(
        own_filled, placed(jnp.arange(own_requests, dtype=jnp.int32) // listed), block_count
    )

    def one_chunk(step, tiles, sb, sf, n, *rest):
        return (jnp.minimum(step, n[0] - 1), 0)

    weights, factor = pl.pallas_call(
        functools.partial(weights_kernel, block_rows, own_rows),
        grid_spec=pltpu.PrefetchScalarGridSpec(
            num_scalar_prefetch=5,
            grid=(chunks,),
            in_specs=[pl.BlockSpec(memory_space=pl.ANY)],
            out_specs=[
                pl.BlockSpec((GROUP * block_rows, own_rows), one_chunk),
                pl.BlockSpec((rows, 128), lambda *a: (0, 0), pipeline_mode=pl.Buffered(1)),
            ],
            scratch_shapes=[
                pltpu.VMEM((rows + block_rows, width), jnp.bfloat16),
                pltpu.VMEM((rows + block_rows, 128), jnp.float32),
                pltpu.SemaphoreType.DMA,
            ],
        ),
        out_shape=[
            jax.ShapeDtypeStruct((slots * block_rows, own_rows), jnp.bfloat16),
            jax.ShapeDtypeStruct((rows, 128), jnp.float32),
        ],
        compiler_params=pltpu.CompilerParams(vmem_limit_bytes=VMEM_BYTES),
        cost_estimate=pl.CostEstimate(
            flops=2 * requests * block_rows * own_rows * width,
            bytes_accessed=rows * width * 2 + slots * block_rows * own_rows * 2,
            transcendentals=requests * block_rows * own_rows,
        ),
        name="weights",
    )(step_tile, slot_block, slot_first, used, counts, memory)

    own_weights = weights.reshape(slots, block_rows, own_rows)[own_slot]
    own_weights = own_weights.reshape(devices * capacity * block_rows, own_rows)
    own_factor = lax.dynamic_slice_in_dim(factor, me * own_rows, own_rows, 0)

    def tile_of(step, tiles, *rest):
        return (tiles[step], 0)

    def late_tile(step, *rest):
        return (jnp.maximum(step - chunks, 0), 0)

    def same(*a):
        return (0, 0)

    outs = []
    for piece, own_piece in zip(priors, own_priors):
        outs.append(
            pl.pallas_call(
                functools.partial(labels_kernel, chunks, block_rows, capacity),
                grid_spec=pltpu.PrefetchScalarGridSpec(
                    num_scalar_prefetch=7,
                    grid=(chunks + devices,),
                    in_specs=[
                        pl.BlockSpec((GROUP * block_rows, own_rows), one_chunk),
                        pl.BlockSpec((capacity * block_rows, own_rows), late_tile),
                        pl.BlockSpec((own_rows, part_width), tile_of),
                        pl.BlockSpec((own_rows, 128), late_tile),
                        pl.BlockSpec((own_rows, part_width), same),
                        pl.BlockSpec((own_rows, 128), same),
                    ],
                    out_specs=pl.BlockSpec((own_rows, part_width), same),
                    scratch_shapes=[
                        pltpu.VMEM((rows + block_rows, part_width), jnp.float32),
                        pltpu.VMEM((own_rows + block_rows, part_width), jnp.float32),
                    ],
                ),
                out_shape=jax.ShapeDtypeStruct((own_rows, part_width), jnp.float32),
                compiler_params=pltpu.CompilerParams(vmem_limit_bytes=VMEM_BYTES),
                cost_estimate=pl.CostEstimate(
                    flops=2 * requests * block_rows * own_rows * part_width,
                    bytes_accessed=slots * block_rows * own_rows * 2,
                    transcendentals=0,
                ),
                name="labels",
            )(
                step_tile, slot_block, slot_first, used, own_block, own_first, me.reshape(1),
                weights, own_weights, piece, factor, own_piece, own_factor,
            )
        )
    return outs[0] if splits == 1 else jnp.concatenate(outs, axis=1)


def solution(mesh):
    in_specs = (P("dp", None), P("tensor"), P("dp", "tensor"), P("dp", None), P("dp"))
    out_specs = P("dp", "tensor")
    return jax.shard_map(
        on_device, mesh=mesh, in_specs=in_specs, out_specs=out_specs, check_vma=False
    )
```

```python
import functools
import math

import jax
import jax.numpy as jnp
from jax import lax
from jax.experimental import pallas as pl
from jax.experimental.pallas import tpu as pltpu
from jax.sharding import PartitionSpec as P

ALPHA = 0.75
SOFTMAX_TEMPER = 0.05
EPSILON = 1e-06
GROUP = 16
VMEM_BYTES = 60 * 1024 * 1024


def unitnorm_rows(features):
    wide = features.astype(jnp.float32)
    scale = lax.rsqrt(jnp.mean(wide * wide, axis=1, keepdims=True) + EPSILON)
    return (wide * scale / math.sqrt(wide.shape[1])).astype(jnp.bfloat16)


def weights_kernel(
    block_rows, tile_rows, step_tile, slot_block, slot_first, used, counts, memory, out, factor,
    held, total, sem
):
    step = pl.program_id(0)
    rows = memory.shape[0]

    @pl.when(step == 0)
    def _():
        copy = pltpu.make_async_copy(memory, held.at[pl.ds(0, rows)], sem)
        copy.start()
        copy.wait()

    @pl.when(step < used[0])
    def _():
        tile = step_tile[step]
        starts = [
            pl.multiple_of(slot_block[step * GROUP + j] * block_rows, block_rows)
            for j in range(GROUP)
        ]
        keys = held[pl.ds(pl.multiple_of(tile * tile_rows, tile_rows), tile_rows), :]
        some = GROUP // 2
        for begin in range(0, GROUP, some):
            queries = jnp.concatenate(
                [held[pl.ds(s, block_rows), :] for s in starts[begin : begin + some]], axis=0
            )
            scores = lax.dot_general(
                queries, keys, (((1,), (1,)), ((), ())), preferred_element_type=jnp.float32
            )
            columns = lax.broadcasted_iota(jnp.int32, scores.shape, 1)
            weights = jnp.where(
                columns < counts[tile], jnp.exp(scores * (1.0 / SOFTMAX_TEMPER)), 0.0
            ).astype(jnp.bfloat16)
            out[begin * block_rows : (begin + some) * block_rows, :] = weights
            sums = jnp.sum(weights.astype(jnp.float32), axis=1, keepdims=True)
            sums = jnp.broadcast_to(sums, (sums.shape[0], 128))
            for j in range(some):
                where = pl.ds(starts[begin + j], block_rows)
                old = jnp.where(slot_first[step * GROUP + begin + j] == 1, 0.0, total[where, :])
                total[where, :] = old + sums[j * block_rows : (j + 1) * block_rows]

    @pl.when(step == pl.num_programs(0) - 1)
    def _():
        factor[...] = ALPHA / total[pl.ds(0, rows), :]


def labels_kernel(
    chunks, block_rows, own_slots, step_tile, slot_block, slot_first, used, own_block, own_first,
    own_slot, me, weights, *rest
):
    own_weights = rest[:own_slots]
    prior, factor, own_prior, own_factor, out, total, own_total = rest[own_slots:]
    step = pl.program_id(0)
    tile_rows, width = prior.shape
    piece = 256 if width % 256 == 0 else 128
    pieces = [slice(p, p + piece) for p in range(0, width, piece)]

    def add(into, part, cut, blocks, firsts, base, number):
        for j in range(number):
            start = pl.multiple_of(blocks[base + j] * block_rows, block_rows)
            where = pl.ds(start, block_rows)
            old = jnp.where(firsts[base + j] == 1, 0.0, into[where, cut])
            into[where, cut] = old + part[j * block_rows : (j + 1) * block_rows]

    def wide(lanes):
        return jnp.concatenate([lanes] * (piece // 128), axis=1)

    @pl.when(step < used[0])
    def _():
        for cut in pieces:
            part = jnp.dot(weights[...], prior[:, cut], preferred_element_type=jnp.float32)
            add(total, part, cut, slot_block, slot_first, step * GROUP, GROUP)

    @pl.when(step >= chunks)
    def _():
        tile = step - chunks
        rows = pl.ds(pl.multiple_of(tile * tile_rows, tile_rows), tile_rows)
        sent = jnp.concatenate([w[...] for w in own_weights], axis=0)
        scale = wide(factor[...])
        for cut in pieces:
            labels = total[rows, cut] * scale + (1.0 - ALPHA) * prior[:, cut].astype(jnp.float32)
            part = jnp.dot(
                sent, labels.astype(jnp.bfloat16), preferred_element_type=jnp.float32
            )
            add(own_total, part, cut, own_block, own_first, tile * own_slots, own_slots)

    @pl.when(step == pl.num_programs(0) - 1)
    def _():
        scale = wide(own_factor[...])
        for cut in pieces:
            spread = own_total[pl.ds(0, tile_rows), cut] * scale
            spread += (1.0 - ALPHA) * own_prior[:, cut].astype(jnp.float32)
            out[:, cut] = jnp.log(spread)


def gather_kernel(features, lists, memory, all_lists, recv, send, local):
    dp, y = lax.axis_index("dp"), lax.axis_index("tensor")
    z, x, c = dp // 4, (dp // 2) % 2, dp % 2
    rows = features.shape[0]
    half = rows // 2

    def index(zz, xx):
        return zz * 4 + xx * 2 + c

    def region(t, kind):
        if kind == 2:
            return all_lists.at[t]
        h = y if kind == 0 else 1 - y
        return memory.at[pl.ds(pl.multiple_of(t * rows + h * half, half), half)]

    def own_region(kind):
        if kind == 2:
            return lists
        h = y if kind == 0 else 1 - y
        return features.at[pl.ds(pl.multiple_of(h * half, half), half)]

    def partner(way):
        if way == 0:
            return {"dp": dp - 4}
        if way == 1:
            return {"dp": dp + 4}
        if way == 2:
            return {"dp": dp + 2 - 4 * x}
        if way == 3:
            return {"tensor": 1 - y}
        return {"dp": dp + 1 - 2 * c}

    def reach(way):
        if way == 0:
            return z > 0
        if way == 1:
            return z < 3
        return None

    def guarded(conditions, body):
        conditions = [q for q in conditions if q is not None]
        if not conditions:
            body()
        else:
            both = conditions[0]
            for q in conditions[1:]:
                both = jnp.logical_and(both, q)
            pl.when(both)(body)

    sent = []

    def copy(zz, xx, kind, way, own):
        t = index(zz, xx)
        arrives = 1 if way == 3 else kind
        return pltpu.make_async_remote_copy(
            src_ref=own_region(kind) if own else region(t, kind),
            dst_ref=region(t, kind),
            send_sem=send.at[zz * 2 + xx, kind, way],
            recv_sem=recv.at[t, arrives],
            device_id=partner(way),
            device_id_type=pl.DeviceIdType.MESH,
        )

    def push(zz, xx, kind, ways, exists=None, own=False):
        for way in ways:
            guards = (exists, reach(way))
            guarded(guards, lambda way=way: copy(zz, xx, kind, way, own).start())
            sent.append((guards, zz, xx, kind, way, own))

    def landed(t, kind):
        pltpu.make_async_remote_copy(
            src_ref=region(t, kind), dst_ref=region(t, kind),
            send_sem=send.at[0, 0, 0], recv_sem=recv.at[t, kind],
            device_id=partner(4), device_id_type=pl.DeviceIdType.MESH,
        ).wait_recv()

    def column(distance):
        if distance == 0:
            return [(z, None, (0, 1))]
        return [
            (z - distance, z >= distance, (1,)),
            (z + distance, z + distance < 4, (0,)),
        ]

    def near(distance, kind):
        for zz, exists, ways in column(distance):
            guarded((exists,), lambda zz=zz: landed(index(zz, x), kind))
            onward = ways + ((2, 3, 4) if kind == 0 else (2, 4))
            push(zz, x, kind, onward, exists)

    def across(distance, kind):
        for zz, exists, _ in column(distance):
            guarded((exists,), lambda zz=zz: landed(index(zz, 1 - x), kind))
            push(zz, 1 - x, kind, (3, 4) if kind == 0 else (4,), exists)

    def mirrored(distance, xx):
        for zz, exists, _ in column(distance):
            guarded((exists,), lambda zz=zz: landed(index(zz, xx), 1))
            push(zz, xx, 1, (4,), exists)

    barrier = pltpu.get_barrier_semaphore()
    for way in range(5):
        guarded(
            (reach(way),),
            lambda way=way: pl.semaphore_signal(
                barrier, inc=1, device_id=partner(way), device_id_type=pl.DeviceIdType.MESH
            ),
        )
    pl.semaphore_wait(barrier, 4 + z * (3 - z) // 2)

    push(z, x, 0, (0, 1, 2, 4), own=True)
    push(z, x, 2, (0, 1, 2, 4), own=True)
    push(z, x, 1, (4,), own=True)
    keep = pl.ds(pl.multiple_of(dp * rows, rows), rows)
    copies = [
        pltpu.make_async_copy(features, memory.at[keep], local.at[0]),
        pltpu.make_async_copy(lists, all_lists.at[dp], local.at[1]),
    ]
    for one in copies:
        one.start()
    for distance in (1, 2, 3):
        for kind in (0, 2):
            near(distance, kind)
        for kind in (0, 2):
            across(distance - 1, kind)
        if distance > 1:
            mirrored(distance - 1, x)
            mirrored(distance - 2, 1 - x)
    for kind in (0, 2):
        across(3, kind)
    mirrored(3, x)
    mirrored(2, 1 - x)
    mirrored(3, 1 - x)
    for zz in range(4):
        for xx in range(2):
            for kind in range(3):
                landed(zz * 4 + xx * 2 + 1 - c, kind)
    for guards, zz, xx, kind, way, own in sent:
        guarded(
            guards,
            lambda zz=zz, xx=xx, kind=kind, way=way, own=own: copy(
                zz, xx, kind, way, own
            ).wait_send(),
        )
    for one in copies:
        one.wait()


def gather_all(normalized, lists, devices):
    rows, width = normalized.shape
    return pl.pallas_call(
        gather_kernel,
        in_specs=[pl.BlockSpec(memory_space=pl.ANY)] * 2,
        out_specs=[pl.BlockSpec(memory_space=pl.ANY)] * 2,
        out_shape=[
            jax.ShapeDtypeStruct((devices * rows, width), normalized.dtype),
            jax.ShapeDtypeStruct((devices,) + lists.shape, lists.dtype),
        ],
        scratch_shapes=[
            pltpu.SemaphoreType.DMA((devices, 3)),
            pltpu.SemaphoreType.DMA((8, 3, 5)),
            pltpu.SemaphoreType.DMA((2,)),
        ],
        compiler_params=pltpu.CompilerParams(collective_id=0, has_side_effects=True),
        cost_estimate=pl.CostEstimate(
            flops=0, bytes_accessed=16 * devices * rows * width * 2, transcendentals=0
        ),
        name="gather",
    )(normalized, lists)


def on_device(features, class_bias, logits, tile_lists, valid_counts):
    devices = lax.axis_size("dp")
    twins = lax.axis_size("tensor")
    own_rows, width = features.shape
    block_count, listed = tile_lists.shape
    block_rows = own_rows // block_count
    rows = own_rows * devices
    blocks = block_count * devices
    requests = blocks * listed
    chunks = (requests + devices * (GROUP - 1)) // GROUP
    slots = chunks * GROUP
    me = lax.axis_index("dp").astype(jnp.int32)
    twin = lax.axis_index("tensor")

    normalized = unitnorm_rows(features)
    adjusted = logits.astype(jnp.float32) + class_bias[None, :]
    exponentials = jnp.exp(adjusted)
    row_totals = lax.psum(jnp.sum(exponentials, axis=1), "tensor")
    prior = (exponentials / row_totals[:, None]).astype(jnp.bfloat16)
    grid_links = devices == 16 and twins == 2
    splits = 1 if grid_links else 2
    part_width = prior.shape[1] // splits
    own_priors = [prior[:, s * part_width : (s + 1) * part_width] for s in range(splits)]
    small = jnp.concatenate([tile_lists.reshape(-1), valid_counts])
    listing = small.shape[0]
    priors = [lax.all_gather(p, "dp", axis=0, tiled=True) for p in own_priors]
    if grid_links:
        lists = jnp.pad(small, (0, 8 * 128 - listing)).reshape(8, 128)
        memory, all_lists = gather_all(normalized, lists, devices)
        small = all_lists.reshape(devices, -1)[:, :listing]
    else:
        share = own_rows // twins
        mine = lax.dynamic_slice_in_dim(normalized, twin * share, share, 0)
        memory = lax.all_gather(mine, ("dp", "tensor"), axis=0, tiled=True)
        small = lax.all_gather(small, "dp", axis=0, tiled=False)
    counts = small[:, -1]
    owners = small[:, :-1].reshape(-1)
    pairs = owners.reshape(-1, listed)
    firsts = jnp.stack([pairs[:, 0] < pairs[:, 1], pairs[:, 1] < pairs[:, 0]], axis=1)
    firsts = firsts.reshape(-1).astype(jnp.int32)
    hits = (owners[:, None] == jnp.arange(devices, dtype=jnp.int32)[None, :]).astype(jnp.int32)
    running = jnp.cumsum(hits, axis=0)
    earlier = jnp.sum((running - hits) * hits, axis=1)
    tile_chunks = (running[-1] + GROUP - 1) // GROUP
    ends = jnp.cumsum(tile_chunks)
    bases = ends - tile_chunks
    position = jnp.sum(hits * bases[None, :], axis=1) * GROUP + earlier
    matches = position[None, :] == jnp.arange(slots, dtype=jnp.int32)[:, None]
    request_ids = jnp.arange(requests, dtype=jnp.int32)
    filled = jnp.any(matches, axis=1)
    source = jnp.sum(jnp.where(matches, request_ids[None, :], 0), axis=1)
    slot_block = jnp.where(filled, source // listed, blocks)
    slot_first = jnp.sum(jnp.where(matches, firsts[None, :], 0), axis=1)
    used = ends[-1:]
    steps = jnp.minimum(jnp.arange(chunks, dtype=jnp.int32), used[0] - 1)
    chunk_tile = jnp.sum((steps[:, None] >= ends[None, :]).astype(jnp.int32), axis=1)
    step_tile = jnp.concatenate([chunk_tile, jnp.arange(devices, dtype=jnp.int32)])

    capacity = max(2, 64 // devices)
    own_requests = block_count * listed
    own_owners = tile_lists.reshape(-1)
    own_hits = (own_owners[:, None] == jnp.arange(devices, dtype=jnp.int32)[None, :]).astype(
        jnp.int32
    )
    own_earlier = jnp.sum((jnp.cumsum(own_hits, axis=0) - own_hits) * own_hits, axis=1)
    own_place = own_owners * capacity + own_earlier
    own_matches = (
        own_place[None, :] == jnp.arange(devices * capacity, dtype=jnp.int32)[:, None]
    )
    own_filled = jnp.any(own_matches, axis=1)

    def placed(values):
        return jnp.sum(jnp.where(own_matches, values[None, :], 0), axis=1)

    own_first = placed(lax.dynamic_slice_in_dim(firsts, me * own_requests, own_requests))
    own_slot = placed(lax.dynamic_slice_in_dim(position, me * own_requests, own_requests))
    own_block = jnp.where(
        own_filled, placed(jnp.arange(own_requests, dtype=jnp.int32) // listed), block_count
    )

    def one_chunk(step, tiles, sb, sf, n, *rest):
        return (jnp.minimum(step, n[0] - 1), 0)

    weights, factor = pl.pallas_call(
        functools.partial(weights_kernel, block_rows, own_rows),
        grid_spec=pltpu.PrefetchScalarGridSpec(
            num_scalar_prefetch=5,
            grid=(chunks,),
            in_specs=[pl.BlockSpec(memory_space=pl.ANY)],
            out_specs=[
                pl.BlockSpec((GROUP * block_rows, own_rows), one_chunk),
                pl.BlockSpec((rows, 128), lambda *a: (0, 0), pipeline_mode=pl.Buffered(1)),
            ],
            scratch_shapes=[
                pltpu.VMEM((rows + block_rows, width), jnp.bfloat16),
                pltpu.VMEM((rows + block_rows, 128), jnp.float32),
                pltpu.SemaphoreType.DMA,
            ],
        ),
        out_shape=[
            jax.ShapeDtypeStruct((slots * block_rows, own_rows), jnp.bfloat16),
            jax.ShapeDtypeStruct((rows, 128), jnp.float32),
        ],
        compiler_params=pltpu.CompilerParams(vmem_limit_bytes=VMEM_BYTES),
        cost_estimate=pl.CostEstimate(
            flops=2 * requests * block_rows * own_rows * width,
            bytes_accessed=rows * width * 2 + slots * block_rows * own_rows * 2,
            transcendentals=requests * block_rows * own_rows,
        ),
        name="weights",
    )(step_tile, slot_block, slot_first, used, counts, memory)

    def tile_of(step, tiles, *rest):
        return (tiles[step], 0)

    def late_tile(step, *rest):
        return (jnp.maximum(step - chunks, 0), 0)

    def same(*a):
        return (0, 0)

    def own_at(j):
        def place(step, tiles, sb, sf, n, ob, of, os, m):
            return (os[jnp.maximum(step - chunks, 0) * capacity + j], 0)

        return pl.BlockSpec((block_rows, own_rows), place)

    def mine_at(step, tiles, sb, sf, n, ob, of, os, m):
        return (m[0], 0)

    outs = []
    for piece, own_piece in zip(priors, own_priors):
        outs.append(
            pl.pallas_call(
                functools.partial(labels_kernel, chunks, block_rows, capacity),
                grid_spec=pltpu.PrefetchScalarGridSpec(
                    num_scalar_prefetch=8,
                    grid=(chunks + devices,),
                    in_specs=[
                        pl.BlockSpec((GROUP * block_rows, own_rows), one_chunk),
                        *[own_at(j) for j in range(capacity)],
                        pl.BlockSpec((own_rows, part_width), tile_of),
                        pl.BlockSpec((own_rows, 128), late_tile),
                        pl.BlockSpec((own_rows, part_width), same),
                        pl.BlockSpec((own_rows, 128), mine_at),
                    ],
                    out_specs=pl.BlockSpec((own_rows, part_width), same),
                    scratch_shapes=[
                        pltpu.VMEM((rows + block_rows, part_width), jnp.float32),
                        pltpu.VMEM((own_rows + block_rows, part_width), jnp.float32),
                    ],
                ),
                out_shape=jax.ShapeDtypeStruct((own_rows, part_width), jnp.float32),
                compiler_params=pltpu.CompilerParams(vmem_limit_bytes=VMEM_BYTES),
                cost_estimate=pl.CostEstimate(
                    flops=2 * requests * block_rows * own_rows * part_width,
                    bytes_accessed=slots * block_rows * own_rows * 2,
                    transcendentals=0,
                ),
                name="labels",
            )(
                step_tile, slot_block, slot_first, used, own_block, own_first, own_slot,
                me.reshape(1), weights, *[weights] * capacity, piece, factor, own_piece, factor,
            )
        )
    return outs[0] if splits == 1 else jnp.concatenate(outs, axis=1)


def solution(mesh):
    in_specs = (P("dp", None), P("tensor"), P("dp", "tensor"), P("dp", None), P("dp"))
    out_specs = P("dp", "tensor")
    return jax.shard_map(
        on_device, mesh=mesh, in_specs=in_specs, out_specs=out_specs, check_vma=False
    )
```

```python
import functools
import math

import jax
import jax.numpy as jnp
from jax import lax
from jax.experimental import pallas as pl
from jax.experimental.pallas import tpu as pltpu
from jax.sharding import PartitionSpec as P

ALPHA = 0.75
SOFTMAX_TEMPER = 0.05
EPSILON = 1e-06
GROUP = 16
VMEM_BYTES = 60 * 1024 * 1024


def unitnorm_rows(features):
    wide = features.astype(jnp.float32)
    scale = lax.rsqrt(jnp.mean(wide * wide, axis=1, keepdims=True) + EPSILON)
    return (wide * scale / math.sqrt(wide.shape[1])).astype(jnp.bfloat16)


def weights_kernel(
    block_rows, tile_rows, step_tile, slot_block, slot_first, used, counts, memory, out, factor,
    held, total, sem
):
    step = pl.program_id(0)
    rows = memory.shape[0]

    @pl.when(step == 0)
    def _():
        copy = pltpu.make_async_copy(memory, held.at[pl.ds(0, rows)], sem)
        copy.start()
        copy.wait()

    @pl.when(step < used[0])
    def _():
        tile = step_tile[step]
        starts = [
            pl.multiple_of(slot_block[step * GROUP + j] * block_rows, block_rows)
            for j in range(GROUP)
        ]
        keys = held[pl.ds(pl.multiple_of(tile * tile_rows, tile_rows), tile_rows), :]
        some = GROUP // 2
        where = [pl.ds(start, block_rows) for start in starts]
        olds = [
            jnp.where(slot_first[step * GROUP + j] == 1, 0.0, total[where[j], :])
            for j in range(GROUP)
        ]
        news = []
        for begin in range(0, GROUP, some):
            queries = jnp.concatenate(
                [held[rows_at, :] for rows_at in where[begin : begin + some]], axis=0
            )
            scores = lax.dot_general(
                queries, keys, (((1,), (1,)), ((), ())), preferred_element_type=jnp.float32
            )
            columns = lax.broadcasted_iota(jnp.int32, scores.shape, 1)
            weights = jnp.where(
                columns < counts[tile], jnp.exp(scores * (1.0 / SOFTMAX_TEMPER)), 0.0
            ).astype(jnp.bfloat16)
            out[begin * block_rows : (begin + some) * block_rows, :] = weights
            sums = jnp.sum(weights.astype(jnp.float32), axis=1, keepdims=True)
            for j in range(some):
                news.append(olds[begin + j] + sums[j * block_rows : (j + 1) * block_rows])
        for j in range(GROUP):
            total[where[j], :] = news[j]

    @pl.when(step == pl.num_programs(0) - 1)
    def _():
        factor[...] = ALPHA / total[pl.ds(0, rows), :]


def labels_kernel(
    chunks, block_rows, own_slots, step_tile, position, used, own_slot, own_place, me, weights,
    *rest
):
    own_weights = rest[:own_slots]
    prior, factor, own_prior, own_factor, out, partial, own_partial = rest[own_slots:]
    step = pl.program_id(0)
    tile_rows, width = prior.shape
    tile_blocks = tile_rows // block_rows
    piece = 256 if width % 256 == 0 else 128
    pieces = [slice(p, p + piece) for p in range(0, width, piece)]

    def summed(source, places, base, cut):
        found = []
        for j in range(tile_blocks):
            pair = [
                source[pl.ds(pl.multiple_of(places[base + 2 * j + k] * block_rows, block_rows),
                             block_rows), cut].astype(jnp.float32)
                for k in range(2)
            ]
            found.append(pair[0] + pair[1])
        return jnp.concatenate(found, axis=0)

    def wide(lanes):
        return jnp.concatenate([lanes] * (piece // 128), axis=1)

    @pl.when(step < used[0])
    def _():
        size = weights.shape[0]
        rows = pl.ds(pl.multiple_of(step * size, size), size)
        for cut in pieces:
            part = jnp.dot(weights[...], prior[:, cut], preferred_element_type=jnp.float32)
            partial[rows, cut] = part.astype(jnp.bfloat16)

    @pl.when(step >= chunks)
    def _():
        tile = step - chunks
        size = own_slots * block_rows
        rows = pl.ds(pl.multiple_of(tile * size, size), size)
        sent = jnp.concatenate([w[...] for w in own_weights], axis=0)
        scale = wide(factor[...])
        for cut in pieces:
            numerator = summed(partial, position, tile * tile_blocks * 2, cut)
            labels = numerator * scale + (1.0 - ALPHA) * prior[:, cut].astype(jnp.float32)
            part = jnp.dot(
                sent, labels.astype(jnp.bfloat16), preferred_element_type=jnp.float32
            )
            own_partial[rows, cut] = part.astype(jnp.bfloat16)

    @pl.when(step == pl.num_programs(0) - 1)
    def _():
        scale = wide(own_factor[...])
        for cut in pieces:
            spread = summed(own_partial, own_place, 0, cut) * scale
            spread += (1.0 - ALPHA) * own_prior[:, cut].astype(jnp.float32)
            out[:, cut] = jnp.log(spread)


def gather_kernel(features, labels, lists, memory, priors, all_lists, recv, send, local):
    dp, y = lax.axis_index("dp"), lax.axis_index("tensor")
    z, x, c = dp // 4, (dp // 2) % 2, dp % 2
    rows = features.shape[0]
    half = rows // 2

    def index(zz, xx):
        return zz * 4 + xx * 2 + c

    def region(t, kind):
        if kind == 3:
            return all_lists.at[t]
        if kind == 2:
            return priors.at[pl.ds(pl.multiple_of(t * rows, rows), rows)]
        h = y if kind == 0 else 1 - y
        return memory.at[pl.ds(pl.multiple_of(t * rows + h * half, half), half)]

    def own_region(kind):
        if kind == 3:
            return lists
        if kind == 2:
            return labels
        h = y if kind == 0 else 1 - y
        return features.at[pl.ds(pl.multiple_of(h * half, half), half)]

    def partner(way):
        if way == 0:
            return {"dp": dp - 4}
        if way == 1:
            return {"dp": dp + 4}
        if way == 2:
            return {"dp": dp + 2 - 4 * x}
        if way == 3:
            return {"tensor": 1 - y}
        return {"dp": dp + 1 - 2 * c}

    def reach(way):
        if way == 0:
            return z > 0
        if way == 1:
            return z < 3
        return None

    def guarded(conditions, body):
        conditions = [q for q in conditions if q is not None]
        if not conditions:
            body()
        else:
            both = conditions[0]
            for q in conditions[1:]:
                both = jnp.logical_and(both, q)
            pl.when(both)(body)

    sent = []

    def copy(zz, xx, kind, way, own):
        t = index(zz, xx)
        arrives = 1 if way == 3 else kind
        return pltpu.make_async_remote_copy(
            src_ref=own_region(kind) if own else region(t, kind),
            dst_ref=region(t, kind),
            send_sem=send.at[zz * 2 + xx, kind, way],
            recv_sem=recv.at[t, arrives],
            device_id=partner(way),
            device_id_type=pl.DeviceIdType.MESH,
        )

    def push(zz, xx, kind, ways, exists=None, own=False):
        for way in ways:
            guards = (exists, reach(way))
            guarded(guards, lambda way=way: copy(zz, xx, kind, way, own).start())
            sent.append((guards, zz, xx, kind, way, own))

    def landed(t, kind):
        pltpu.make_async_remote_copy(
            src_ref=region(t, kind), dst_ref=region(t, kind),
            send_sem=send.at[0, 0, 0], recv_sem=recv.at[t, kind],
            device_id=partner(4), device_id_type=pl.DeviceIdType.MESH,
        ).wait_recv()

    def column(distance):
        if distance == 0:
            return [(z, None, (0, 1))]
        return [
            (z - distance, z >= distance, (1,)),
            (z + distance, z + distance < 4, (0,)),
        ]

    def near(distance, kind):
        for zz, exists, ways in column(distance):
            guarded((exists,), lambda zz=zz: landed(index(zz, x), kind))
            onward = ways + ((2, 3, 4) if kind == 0 else (2, 4))
            push(zz, x, kind, onward, exists)

    def across(distance, kind):
        for zz, exists, _ in column(distance):
            guarded((exists,), lambda zz=zz: landed(index(zz, 1 - x), kind))
            push(zz, 1 - x, kind, (3, 4) if kind == 0 else (4,), exists)

    def mirrored(distance, xx):
        for zz, exists, _ in column(distance):
            guarded((exists,), lambda zz=zz: landed(index(zz, xx), 1))
            push(zz, xx, 1, (4,), exists)

    barrier = pltpu.get_barrier_semaphore()
    for way in range(5):
        guarded(
            (reach(way),),
            lambda way=way: pl.semaphore_signal(
                barrier, inc=1, device_id=partner(way), device_id_type=pl.DeviceIdType.MESH
            ),
        )
    pl.semaphore_wait(barrier, 4 + z * (3 - z) // 2)

    push(z, x, 0, (0, 1, 2, 4), own=True)
    push(z, x, 3, (0, 1, 2, 4), own=True)
    keep = pl.ds(pl.multiple_of(dp * rows, rows), rows)
    copies = [
        pltpu.make_async_copy(features, memory.at[keep], local.at[0]),
        pltpu.make_async_copy(labels, priors.at[keep], local.at[1]),
        pltpu.make_async_copy(lists, all_lists.at[dp], local.at[2]),
    ]
    for one in copies:
        one.start()
    for distance in (1, 2, 3):
        near(distance, 0)
        across(distance - 1, 0)
        near(distance, 3)
        across(distance - 1, 3)
        if distance == 2:
            push(z, x, 2, (0, 1, 2, 4), own=True)
            push(z, x, 1, (4,), own=True)
    across(3, 0)
    across(3, 3)
    for distance in (1, 2, 3):
        near(distance, 2)
        across(distance - 1, 2)
        mirrored(distance, x)
        mirrored(distance - 1, 1 - x)
    mirrored(3, 1 - x)
    across(3, 2)
    for zz in range(4):
        for xx in range(2):
            for kind in range(4):
                landed(zz * 4 + xx * 2 + 1 - c, kind)
    for guards, zz, xx, kind, way, own in sent:
        guarded(
            guards,
            lambda zz=zz, xx=xx, kind=kind, way=way, own=own: copy(
                zz, xx, kind, way, own
            ).wait_send(),
        )
    for one in copies:
        one.wait()


def gather_all(normalized, prior, lists, devices):
    rows, width = normalized.shape
    classes = prior.shape[1]
    return pl.pallas_call(
        gather_kernel,
        in_specs=[pl.BlockSpec(memory_space=pl.ANY)] * 3,
        out_specs=[pl.BlockSpec(memory_space=pl.ANY)] * 3,
        out_shape=[
            jax.ShapeDtypeStruct((devices * rows, width), normalized.dtype),
            jax.ShapeDtypeStruct((devices * rows, classes), prior.dtype),
            jax.ShapeDtypeStruct((devices,) + lists.shape, lists.dtype),
        ],
        scratch_shapes=[
            pltpu.SemaphoreType.DMA((devices, 4)),
            pltpu.SemaphoreType.DMA((8, 4, 5)),
            pltpu.SemaphoreType.DMA((3,)),
        ],
        compiler_params=pltpu.CompilerParams(collective_id=0, has_side_effects=True),
        cost_estimate=pl.CostEstimate(
            flops=0, bytes_accessed=2 * devices * rows * (width + classes) * 2, transcendentals=0
        ),
        name="gather",
    )(normalized, prior, lists)


def on_device(features, class_bias, logits, tile_lists, valid_counts):
    devices = lax.axis_size("dp")
    twins = lax.axis_size("tensor")
    own_rows, width = features.shape
    block_count, listed = tile_lists.shape
    block_rows = own_rows // block_count
    rows = own_rows * devices
    blocks = block_count * devices
    requests = blocks * listed
    chunks = (requests + devices * (GROUP - 1)) // GROUP
    slots = chunks * GROUP
    me = lax.axis_index("dp").astype(jnp.int32)
    twin = lax.axis_index("tensor")

    normalized = unitnorm_rows(features)
    adjusted = logits.astype(jnp.float32) + class_bias[None, :]
    exponentials = jnp.exp(adjusted)
    row_totals = lax.psum(jnp.sum(exponentials, axis=1), "tensor")
    prior = (exponentials / row_totals[:, None]).astype(jnp.bfloat16)
    grid_links = devices == 16 and twins == 2
    splits = 1 if grid_links else 2
    part_width = prior.shape[1] // splits
    own_priors = [prior[:, s * part_width : (s + 1) * part_width] for s in range(splits)]
    small = jnp.concatenate([tile_lists.reshape(-1), valid_counts])
    listing = small.shape[0]
    if grid_links:
        lists = jnp.pad(small, (0, 8 * 128 - listing)).reshape(8, 128)
        memory, gathered, all_lists = gather_all(normalized, prior, lists, devices)
        priors = [gathered]
        small = all_lists.reshape(devices, -1)[:, :listing]
    else:
        share = own_rows // twins
        mine = lax.dynamic_slice_in_dim(normalized, twin * share, share, 0)
        memory = lax.all_gather(mine, ("dp", "tensor"), axis=0, tiled=True)
        small = lax.all_gather(small, "dp", axis=0, tiled=False)
        priors = [lax.all_gather(p, "dp", axis=0, tiled=True) for p in own_priors]
    counts = small[:, -1]
    owners = small[:, :-1].reshape(-1)
    pairs = owners.reshape(-1, listed)
    firsts = jnp.stack([pairs[:, 0] < pairs[:, 1], pairs[:, 1] < pairs[:, 0]], axis=1)
    firsts = firsts.reshape(-1).astype(jnp.int32)
    hits = (owners[:, None] == jnp.arange(devices, dtype=jnp.int32)[None, :]).astype(jnp.int32)
    running = jnp.cumsum(hits, axis=0)
    earlier = jnp.sum((running - hits) * hits, axis=1)
    tile_chunks = (running[-1] + GROUP - 1) // GROUP
    ends = jnp.cumsum(tile_chunks)
    bases = ends - tile_chunks
    position = jnp.sum(hits * bases[None, :], axis=1) * GROUP + earlier
    matches = position[None, :] == jnp.arange(slots, dtype=jnp.int32)[:, None]
    request_ids = jnp.arange(requests, dtype=jnp.int32)
    filled = jnp.any(matches, axis=1)
    source = jnp.sum(jnp.where(matches, request_ids[None, :], 0), axis=1)
    slot_block = jnp.where(filled, source // listed, blocks)
    slot_first = jnp.sum(jnp.where(matches, firsts[None, :], 0), axis=1)
    used = ends[-1:]
    steps = jnp.minimum(jnp.arange(chunks, dtype=jnp.int32), used[0] - 1)
    chunk_tile = jnp.sum((steps[:, None] >= ends[None, :]).astype(jnp.int32), axis=1)
    step_tile = jnp.concatenate([chunk_tile, jnp.arange(devices, dtype=jnp.int32)])

    capacity = max(2, 64 // devices)
    own_requests = block_count * listed
    own_owners = tile_lists.reshape(-1)
    own_hits = (own_owners[:, None] == jnp.arange(devices, dtype=jnp.int32)[None, :]).astype(
        jnp.int32
    )
    own_earlier = jnp.sum((jnp.cumsum(own_hits, axis=0) - own_hits) * own_hits, axis=1)
    own_place = own_owners * capacity + own_earlier
    own_matches = (
        own_place[None, :] == jnp.arange(devices * capacity, dtype=jnp.int32)[:, None]
    )

    def placed(values):
        return jnp.sum(jnp.where(own_matches, values[None, :], 0), axis=1)

    own_slot = placed(lax.dynamic_slice_in_dim(position, me * own_requests, own_requests))

    def one_chunk(step, tiles, sb, sf, n, *rest):
        return (jnp.minimum(step, n[0] - 1), 0)

    weights, factor = pl.pallas_call(
        functools.partial(weights_kernel, block_rows, own_rows),
        grid_spec=pltpu.PrefetchScalarGridSpec(
            num_scalar_prefetch=5,
            grid=(chunks,),
            in_specs=[pl.BlockSpec(memory_space=pl.ANY)],
            out_specs=[
                pl.BlockSpec((GROUP * block_rows, own_rows), one_chunk),
                pl.BlockSpec((rows, 128), lambda *a: (0, 0), pipeline_mode=pl.Buffered(1)),
            ],
            scratch_shapes=[
                pltpu.VMEM((rows + block_rows, width), jnp.bfloat16),
                pltpu.VMEM((rows + block_rows, 128), jnp.float32),
                pltpu.SemaphoreType.DMA,
            ],
        ),
        out_shape=[
            jax.ShapeDtypeStruct((slots * block_rows, own_rows), jnp.bfloat16),
            jax.ShapeDtypeStruct((rows, 128), jnp.float32),
        ],
        compiler_params=pltpu.CompilerParams(vmem_limit_bytes=VMEM_BYTES),
        cost_estimate=pl.CostEstimate(
            flops=2 * requests * block_rows * own_rows * width,
            bytes_accessed=rows * width * 2 + slots * block_rows * own_rows * 2,
            transcendentals=requests * block_rows * own_rows,
        ),
        name="weights",
    )(step_tile, slot_block, slot_first, used, counts, memory)

    def tile_of(step, tiles, *rest):
        return (tiles[step], 0)

    def late_tile(step, *rest):
        return (jnp.maximum(step - chunks, 0), 0)

    def same(*a):
        return (0, 0)

    def used_chunk(step, tiles, ps, n, *rest):
        return (jnp.minimum(step, n[0] - 1), 0)

    def own_at(j):
        def place(step, tiles, ps, n, os, op, m):
            return (os[jnp.maximum(step - chunks, 0) * capacity + j], 0)

        return pl.BlockSpec((block_rows, own_rows), place)

    def mine_at(step, tiles, ps, n, os, op, m):
        return (m[0], 0)

    outs = []
    for piece, own_piece in zip(priors, own_priors):
        outs.append(
            pl.pallas_call(
                functools.partial(labels_kernel, chunks, block_rows, capacity),
                grid_spec=pltpu.PrefetchScalarGridSpec(
                    num_scalar_prefetch=6,
                    grid=(chunks + devices,),
                    in_specs=[
                        pl.BlockSpec((GROUP * block_rows, own_rows), used_chunk),
                        *[own_at(j) for j in range(capacity)],
                        pl.BlockSpec((own_rows, part_width), tile_of),
                        pl.BlockSpec((own_rows, 128), late_tile),
                        pl.BlockSpec((own_rows, part_width), same),
                        pl.BlockSpec((own_rows, 128), mine_at),
                    ],
                    out_specs=pl.BlockSpec((own_rows, part_width), same),
                    scratch_shapes=[
                        pltpu.VMEM((slots * block_rows, part_width), jnp.bfloat16),
                        pltpu.VMEM(
                            (devices * capacity * block_rows, part_width), jnp.bfloat16
                        ),
                    ],
                ),
                out_shape=jax.ShapeDtypeStruct((own_rows, part_width), jnp.float32),
                compiler_params=pltpu.CompilerParams(vmem_limit_bytes=VMEM_BYTES),
                cost_estimate=pl.CostEstimate(
                    flops=2 * requests * block_rows * own_rows * part_width,
                    bytes_accessed=slots * block_rows * own_rows * 2,
                    transcendentals=0,
                ),
                name="labels",
            )(
                step_tile, position, used, own_slot, own_place, me.reshape(1), weights, *[weights] * capacity,
                piece, factor, own_piece, factor,
            )
        )
    return outs[0] if splits == 1 else jnp.concatenate(outs, axis=1)


def solution(mesh):
    in_specs = (P("dp", None), P("tensor"), P("dp", "tensor"), P("dp", None), P("dp"))
    out_specs = P("dp", "tensor")
    return jax.shard_map(
        on_device, mesh=mesh, in_specs=in_specs, out_specs=out_specs, check_vma=False
    )
```

```python
import functools
import math

import jax
import jax.numpy as jnp
from jax import lax
from jax.experimental import pallas as pl
from jax.experimental.pallas import tpu as pltpu
from jax.sharding import PartitionSpec as P

ALPHA = 0.75
SOFTMAX_TEMPER = 0.05
EPSILON = 1e-06
GROUP = 16
VMEM_BYTES = 60 * 1024 * 1024


def unitnorm_rows(features):
    wide = features.astype(jnp.float32)
    scale = lax.rsqrt(jnp.mean(wide * wide, axis=1, keepdims=True) + EPSILON)
    return (wide * scale / math.sqrt(wide.shape[1])).astype(jnp.bfloat16)


def weights_kernel(
    block_rows, tile_rows, step_tile, slot_block, slot_first, used, counts, memory, out, factor,
    held, total, sem
):
    step = pl.program_id(0)
    rows = memory.shape[0]

    @pl.when(step == 0)
    def _():
        copy = pltpu.make_async_copy(memory, held.at[pl.ds(0, rows)], sem)
        copy.start()
        copy.wait()

    @pl.when(step < used[0])
    def _():
        tile = step_tile[step]
        starts = [
            pl.multiple_of(slot_block[step * GROUP + j] * block_rows, block_rows)
            for j in range(GROUP)
        ]
        keys = held[pl.ds(pl.multiple_of(tile * tile_rows, tile_rows), tile_rows), :]
        some = GROUP // 2
        where = [pl.ds(start, block_rows) for start in starts]
        olds = [
            jnp.where(slot_first[step * GROUP + j] == 1, 0.0, total[where[j], :])
            for j in range(GROUP)
        ]
        news = []
        for begin in range(0, GROUP, some):
            queries = jnp.concatenate(
                [held[rows_at, :] for rows_at in where[begin : begin + some]], axis=0
            )
            scores = lax.dot_general(
                queries, keys, (((1,), (1,)), ((), ())), preferred_element_type=jnp.float32
            )
            columns = lax.broadcasted_iota(jnp.int32, scores.shape, 1)
            weights = jnp.where(
                columns < counts[tile], jnp.exp(scores * (1.0 / SOFTMAX_TEMPER)), 0.0
            ).astype(jnp.bfloat16)
            out[begin * block_rows : (begin + some) * block_rows, :] = weights
            sums = jnp.sum(weights.astype(jnp.float32), axis=1, keepdims=True)
            for j in range(some):
                news.append(olds[begin + j] + sums[j * block_rows : (j + 1) * block_rows])
        for j in range(GROUP):
            total[where[j], :] = news[j]

    @pl.when(step == pl.num_programs(0) - 1)
    def _():
        factor[...] = ALPHA / total[pl.ds(0, rows), :]


def labels_kernel(
    chunks, block_rows, own_slots, step_tile, position, used, own_slot, own_place, me,
    all_weights, all_priors, factor, own_factor, out, partial, own_partial, own_weights, prior,
    ring, sem, prior_sems, ring_sems
):
    step = pl.program_id(0)
    tile_rows, width = out.shape
    tiles = prior.shape[0] // tile_rows
    size = ring.shape[1]
    depth = ring.shape[0]
    tile_blocks = tile_rows // block_rows
    piece = 256 if width % 256 == 0 else 128
    pieces = [slice(p, p + piece) for p in range(0, width, piece)]

    def summed(source, places, base, cut):
        found = []
        for j in range(tile_blocks):
            pair = [
                source[pl.ds(pl.multiple_of(places[base + 2 * j + k] * block_rows, block_rows),
                             block_rows), cut].astype(jnp.float32)
                for k in range(2)
            ]
            found.append(pair[0] + pair[1])
        return jnp.concatenate(found, axis=0)

    def wide(lanes):
        return jnp.concatenate([lanes] * (piece // 128), axis=1)

    def prior_rows(tile):
        return pl.ds(pl.multiple_of(tile * tile_rows, tile_rows), tile_rows)

    def prior_copy(tile):
        return pltpu.make_async_copy(
            all_priors.at[prior_rows(tile)], prior.at[prior_rows(tile)], prior_sems.at[tile]
        )

    def ring_copy(chunk):
        return pltpu.make_async_copy(
            all_weights.at[pl.ds(pl.multiple_of(chunk * size, size), size)],
            ring.at[chunk % depth],
            ring_sems.at[chunk % depth],
        )

    def fetch(chunk):
        @pl.when(chunk < used[0])
        def _():
            ring_copy(chunk).start()

    @pl.when(step == 0)
    def _():
        fetch(0)

        @pl.loop(0, tiles)
        def _(tile):
            prior_copy(tile).start()

        for chunk in range(1, depth - 1):
            fetch(chunk)

        @pl.loop(0, own_weights.shape[0] // block_rows)
        def _(i):
            start = pl.multiple_of(own_slot[i] * block_rows, block_rows)
            pltpu.make_async_copy(
                all_weights.at[pl.ds(start, block_rows)],
                own_weights.at[pl.ds(pl.multiple_of(i * block_rows, block_rows), block_rows)],
                sem,
            ).start()

    before = jnp.where(step == 0, -1, step_tile[jnp.maximum(step - 1, 0)])

    @pl.when(step == chunks)
    def _():
        pltpu.make_async_copy(
            all_weights.at[pl.ds(0, own_weights.shape[0])], own_weights, sem
        ).wait()

        @pl.loop(before + 1, tiles)
        def _(tile):
            prior_copy(tile).wait()

    @pl.when(step < used[0])
    def _():
        fetch(step + depth - 1)

        @pl.loop(before + 1, step_tile[step] + 1)
        def _(tile):
            prior_copy(tile).wait()

        ring_copy(step).wait()
        rows = pl.ds(pl.multiple_of(step * size, size), size)
        weights = ring[step % depth]
        for cut in pieces:
            part = jnp.dot(
                weights, prior[prior_rows(step_tile[step]), cut],
                preferred_element_type=jnp.float32,
            )
            partial[rows, cut] = part.astype(jnp.bfloat16)

    @pl.when(step >= chunks)
    def _():
        tile = step - chunks
        count = own_slots * block_rows
        rows = pl.ds(pl.multiple_of(tile * count, count), count)
        sent = own_weights[rows, :]
        scale = wide(factor[...])
        for cut in pieces:
            numerator = summed(partial, position, tile * tile_blocks * 2, cut)
            labels = numerator * scale
            labels += (1.0 - ALPHA) * prior[prior_rows(tile), cut].astype(jnp.float32)
            part = jnp.dot(
                sent, labels.astype(jnp.bfloat16), preferred_element_type=jnp.float32
            )
            own_partial[rows, cut] = part.astype(jnp.bfloat16)

    @pl.when(step == pl.num_programs(0) - 1)
    def _():
        scale = wide(own_factor[...])
        for cut in pieces:
            spread = summed(own_partial, own_place, 0, cut) * scale
            spread += (1.0 - ALPHA) * prior[prior_rows(me[0]), cut].astype(jnp.float32)
            out[:, cut] = jnp.log(spread)


def gather_kernel(
    features, logits, bias, lists, memory, priors, all_lists, labels, raised, sums, twin_sums,
    recv, send, local, sums_sent, sums_came
):
    dp, y = lax.axis_index("dp"), lax.axis_index("tensor")
    z, x, c = dp // 4, (dp // 2) % 2, dp % 2
    rows = features.shape[0]
    half = rows // 2

    def index(zz, xx):
        return zz * 4 + xx * 2 + c

    def region(t, kind):
        if kind == 3:
            return all_lists.at[t]
        if kind == 2:
            return priors.at[pl.ds(pl.multiple_of(t * rows, rows), rows)]
        h = y if kind == 0 else 1 - y
        return memory.at[pl.ds(pl.multiple_of(t * rows + h * half, half), half)]

    def own_region(kind):
        if kind == 3:
            return lists
        if kind == 2:
            return labels
        h = y if kind == 0 else 1 - y
        return features.at[pl.ds(pl.multiple_of(h * half, half), half)]

    def partner(way):
        if way == 0:
            return {"dp": dp - 4}
        if way == 1:
            return {"dp": dp + 4}
        if way == 2:
            return {"dp": dp + 2 - 4 * x}
        if way == 3:
            return {"tensor": 1 - y}
        return {"dp": dp + 1 - 2 * c}

    def reach(way):
        if way == 0:
            return z > 0
        if way == 1:
            return z < 3
        return None

    def guarded(conditions, body):
        conditions = [q for q in conditions if q is not None]
        if not conditions:
            body()
        else:
            both = conditions[0]
            for q in conditions[1:]:
                both = jnp.logical_and(both, q)
            pl.when(both)(body)

    sent = []

    def copy(zz, xx, kind, way, own):
        t = index(zz, xx)
        arrives = 1 if way == 3 else kind
        return pltpu.make_async_remote_copy(
            src_ref=own_region(kind) if own else region(t, kind),
            dst_ref=region(t, kind),
            send_sem=send.at[zz * 2 + xx, kind, way],
            recv_sem=recv.at[t, arrives],
            device_id=partner(way),
            device_id_type=pl.DeviceIdType.MESH,
        )

    def push(zz, xx, kind, ways, exists=None, own=False):
        for way in ways:
            guards = (exists, reach(way))
            guarded(guards, lambda way=way: copy(zz, xx, kind, way, own).start())
            sent.append((guards, zz, xx, kind, way, own))

    def landed(t, kind):
        pltpu.make_async_remote_copy(
            src_ref=region(t, kind), dst_ref=region(t, kind),
            send_sem=send.at[0, 0, 0], recv_sem=recv.at[t, kind],
            device_id=partner(4), device_id_type=pl.DeviceIdType.MESH,
        ).wait_recv()

    def column(distance):
        if distance == 0:
            return [(z, None, (0, 1))]
        return [
            (z - distance, z >= distance, (1,)),
            (z + distance, z + distance < 4, (0,)),
        ]

    def near(distance, kind):
        for zz, exists, ways in column(distance):
            guarded((exists,), lambda zz=zz: landed(index(zz, x), kind))
            onward = ways + ((2, 3, 4) if kind == 0 else (2, 4))
            push(zz, x, kind, onward, exists)

    def across(distance, kind):
        for zz, exists, _ in column(distance):
            guarded((exists,), lambda zz=zz: landed(index(zz, 1 - x), kind))
            push(zz, 1 - x, kind, (3, 4) if kind == 0 else (4,), exists)

    def mirrored(distance, xx):
        for zz, exists, _ in column(distance):
            guarded((exists,), lambda zz=zz: landed(index(zz, xx), 1))
            push(zz, xx, 1, (4,), exists)

    barrier = pltpu.get_barrier_semaphore()
    for way in range(5):
        guarded(
            (reach(way),),
            lambda way=way: pl.semaphore_signal(
                barrier, inc=1, device_id=partner(way), device_id_type=pl.DeviceIdType.MESH
            ),
        )
    pl.semaphore_wait(barrier, 4 + z * (3 - z) // 2)

    push(z, x, 0, (0, 1, 2, 4), own=True)
    push(z, x, 3, (0, 1, 2, 4), own=True)
    keep = pl.ds(pl.multiple_of(dp * rows, rows), rows)
    copies = [
        pltpu.make_async_copy(features, memory.at[keep], local.at[0]),
        pltpu.make_async_copy(lists, all_lists.at[dp], local.at[1]),
        pltpu.make_async_copy(labels, priors.at[keep], local.at[2]),
    ]
    for one in copies[:2]:
        one.start()
    slab = 64

    @pl.loop(0, rows // slab)
    def _(i):
        at = pl.ds(pl.multiple_of(i * slab, slab), slab)
        grown = jnp.exp(logits[at, :].astype(jnp.float32) + bias[...])
        raised[at, :] = grown
        sums[at, :] = jnp.broadcast_to(jnp.sum(grown, axis=1, keepdims=True), (slab, 128))

    swap = pltpu.make_async_remote_copy(
        src_ref=sums, dst_ref=twin_sums, send_sem=sums_sent, recv_sem=sums_came,
        device_id=partner(3), device_id_type=pl.DeviceIdType.MESH,
    )
    swap.start()
    swap.wait()

    @pl.loop(0, rows // slab)
    def _(i):
        at = pl.ds(pl.multiple_of(i * slab, slab), slab)
        whole = sums[at, :] + twin_sums[at, :]
        whole = jnp.concatenate([whole] * (raised.shape[1] // 128), axis=1)
        labels[at, :] = (raised[at, :] / whole).astype(jnp.bfloat16)

    copies[2].start()
    for distance in (1, 2, 3):
        near(distance, 0)
        across(distance - 1, 0)
        near(distance, 3)
        across(distance - 1, 3)
        if distance == 2:
            push(z, x, 2, (0, 1, 2, 4), own=True)
            push(z, x, 1, (4,), own=True)
    across(3, 0)
    across(3, 3)
    for distance in (1, 2, 3):
        near(distance, 2)
        across(distance - 1, 2)
        mirrored(distance, x)
        mirrored(distance - 1, 1 - x)
    mirrored(3, 1 - x)
    across(3, 2)
    for zz in range(4):
        for xx in range(2):
            for kind in range(4):
                landed(zz * 4 + xx * 2 + 1 - c, kind)
    for guards, zz, xx, kind, way, own in sent:
        guarded(
            guards,
            lambda zz=zz, xx=xx, kind=kind, way=way, own=own: copy(
                zz, xx, kind, way, own
            ).wait_send(),
        )
    for one in copies:
        one.wait()


def gather_all(normalized, logits, bias, lists, devices):
    rows, width = normalized.shape
    classes = logits.shape[1]
    return pl.pallas_call(
        gather_kernel,
        in_specs=[
            pl.BlockSpec(memory_space=pl.ANY),
            pl.BlockSpec(memory_space=pltpu.VMEM),
            pl.BlockSpec(memory_space=pltpu.VMEM),
            pl.BlockSpec(memory_space=pl.ANY),
        ],
        out_specs=[pl.BlockSpec(memory_space=pl.ANY)] * 3,
        out_shape=[
            jax.ShapeDtypeStruct((devices * rows, width), normalized.dtype),
            jax.ShapeDtypeStruct((devices * rows, classes), jnp.bfloat16),
            jax.ShapeDtypeStruct((devices,) + lists.shape, lists.dtype),
        ],
        scratch_shapes=[
            pltpu.VMEM((rows, classes), jnp.bfloat16),
            pltpu.VMEM((rows, classes), jnp.float32),
            pltpu.VMEM((rows, 128), jnp.float32),
            pltpu.VMEM((rows, 128), jnp.float32),
            pltpu.SemaphoreType.DMA((devices, 4)),
            pltpu.SemaphoreType.DMA((8, 4, 5)),
            pltpu.SemaphoreType.DMA((3,)),
            pltpu.SemaphoreType.DMA,
            pltpu.SemaphoreType.DMA,
        ],
        compiler_params=pltpu.CompilerParams(
            collective_id=0, has_side_effects=True, vmem_limit_bytes=VMEM_BYTES // 3
        ),
        cost_estimate=pl.CostEstimate(
            flops=0, bytes_accessed=2 * devices * rows * (width + classes) * 2, transcendentals=0
        ),
        name="gather",
    )(normalized, logits, bias, lists)


def on_device(features, class_bias, logits, tile_lists, valid_counts):
    devices = lax.axis_size("dp")
    twins = lax.axis_size("tensor")
    own_rows, width = features.shape
    block_count, listed = tile_lists.shape
    block_rows = own_rows // block_count
    rows = own_rows * devices
    blocks = block_count * devices
    requests = blocks * listed
    chunks = (requests + devices * (GROUP - 1)) // GROUP
    slots = chunks * GROUP
    me = lax.axis_index("dp").astype(jnp.int32)
    twin = lax.axis_index("tensor")

    normalized = unitnorm_rows(features)
    grid_links = devices == 16 and twins == 2
    splits = 1 if grid_links else 2
    part_width = logits.shape[1] // splits
    small = jnp.concatenate([tile_lists.reshape(-1), valid_counts])
    listing = small.shape[0]
    if grid_links:
        lists = jnp.pad(small, (0, 8 * 128 - listing)).reshape(8, 128)
        memory, gathered, all_lists = gather_all(
            normalized, logits, class_bias[None, :], lists, devices
        )
        priors = [gathered]
        small = all_lists.reshape(devices, -1)[:, :listing]
    else:
        adjusted = logits.astype(jnp.float32) + class_bias[None, :]
        exponentials = jnp.exp(adjusted)
        row_totals = lax.psum(jnp.sum(exponentials, axis=1), "tensor")
        prior = (exponentials / row_totals[:, None]).astype(jnp.bfloat16)
        own_priors = [prior[:, s * part_width : (s + 1) * part_width] for s in range(splits)]
        share = own_rows // twins
        mine = lax.dynamic_slice_in_dim(normalized, twin * share, share, 0)
        memory = lax.all_gather(mine, ("dp", "tensor"), axis=0, tiled=True)
        small = lax.all_gather(small, "dp", axis=0, tiled=False)
        priors = [lax.all_gather(p, "dp", axis=0, tiled=True) for p in own_priors]
    counts = small[:, -1]
    owners = small[:, :-1].reshape(-1)
    pairs = owners.reshape(-1, listed)
    firsts = jnp.stack([pairs[:, 0] < pairs[:, 1], pairs[:, 1] < pairs[:, 0]], axis=1)
    firsts = firsts.reshape(-1).astype(jnp.int32)
    hits = (owners[:, None] == jnp.arange(devices, dtype=jnp.int32)[None, :]).astype(jnp.int32)
    running = jnp.cumsum(hits, axis=0)
    earlier = jnp.sum((running - hits) * hits, axis=1)
    tile_chunks = (running[-1] + GROUP - 1) // GROUP
    ends = jnp.cumsum(tile_chunks)
    bases = ends - tile_chunks
    position = jnp.sum(hits * bases[None, :], axis=1) * GROUP + earlier
    matches = position[None, :] == jnp.arange(slots, dtype=jnp.int32)[:, None]
    request_ids = jnp.arange(requests, dtype=jnp.int32)
    filled = jnp.any(matches, axis=1)
    source = jnp.sum(jnp.where(matches, request_ids[None, :], 0), axis=1)
    slot_block = jnp.where(filled, source // listed, blocks)
    slot_first = jnp.sum(jnp.where(matches, firsts[None, :], 0), axis=1)
    used = ends[-1:]
    steps = jnp.minimum(jnp.arange(chunks, dtype=jnp.int32), used[0] - 1)
    chunk_tile = jnp.sum((steps[:, None] >= ends[None, :]).astype(jnp.int32), axis=1)
    step_tile = jnp.concatenate([chunk_tile, jnp.arange(devices, dtype=jnp.int32)])

    capacity = max(2, 64 // devices)
    own_requests = block_count * listed
    own_owners = tile_lists.reshape(-1)
    own_hits = (own_owners[:, None] == jnp.arange(devices, dtype=jnp.int32)[None, :]).astype(
        jnp.int32
    )
    own_earlier = jnp.sum((jnp.cumsum(own_hits, axis=0) - own_hits) * own_hits, axis=1)
    own_place = own_owners * capacity + own_earlier
    own_matches = (
        own_place[None, :] == jnp.arange(devices * capacity, dtype=jnp.int32)[:, None]
    )

    def placed(values):
        return jnp.sum(jnp.where(own_matches, values[None, :], 0), axis=1)

    own_slot = placed(lax.dynamic_slice_in_dim(position, me * own_requests, own_requests))

    def one_chunk(step, tiles, sb, sf, n, *rest):
        return (jnp.minimum(step, n[0] - 1), 0)

    weights, factor = pl.pallas_call(
        functools.partial(weights_kernel, block_rows, own_rows),
        grid_spec=pltpu.PrefetchScalarGridSpec(
            num_scalar_prefetch=5,
            grid=(chunks,),
            in_specs=[pl.BlockSpec(memory_space=pl.ANY)],
            out_specs=[
                pl.BlockSpec((GROUP * block_rows, own_rows), one_chunk),
                pl.BlockSpec((rows, 128), lambda *a: (0, 0), pipeline_mode=pl.Buffered(1)),
            ],
            scratch_shapes=[
                pltpu.VMEM((rows + block_rows, width), jnp.bfloat16),
                pltpu.VMEM((rows + block_rows, 128), jnp.float32),
                pltpu.SemaphoreType.DMA,
            ],
        ),
        out_shape=[
            jax.ShapeDtypeStruct((slots * block_rows, own_rows), jnp.bfloat16),
            jax.ShapeDtypeStruct((rows, 128), jnp.float32),
        ],
        compiler_params=pltpu.CompilerParams(vmem_limit_bytes=VMEM_BYTES),
        cost_estimate=pl.CostEstimate(
            flops=2 * requests * block_rows * own_rows * width,
            bytes_accessed=rows * width * 2 + slots * block_rows * own_rows * 2,
            transcendentals=requests * block_rows * own_rows,
        ),
        name="weights",
    )(step_tile, slot_block, slot_first, used, counts, memory)

    def late_tile(step, *rest):
        return (jnp.maximum(step - chunks, 0), 0)

    def same(*a):
        return (0, 0)

    def mine_at(step, tiles, ps, n, os, op, m):
        return (m[0], 0)

    outs = []
    for piece in priors:
        outs.append(
            pl.pallas_call(
                functools.partial(labels_kernel, chunks, block_rows, capacity),
                grid_spec=pltpu.PrefetchScalarGridSpec(
                    num_scalar_prefetch=6,
                    grid=(chunks + devices,),
                    in_specs=[
                        pl.BlockSpec(memory_space=pl.ANY),
                        pl.BlockSpec(memory_space=pl.ANY),
                        pl.BlockSpec((own_rows, 128), late_tile),
                        pl.BlockSpec(
                            (own_rows, 128), mine_at, pipeline_mode=pl.Buffered(1)
                        ),
                    ],
                    out_specs=pl.BlockSpec(
                        (own_rows, part_width), same, pipeline_mode=pl.Buffered(1)
                    ),
                    scratch_shapes=[
                        pltpu.VMEM((slots * block_rows, part_width), jnp.bfloat16),
                        pltpu.VMEM(
                            (devices * capacity * block_rows, part_width), jnp.bfloat16
                        ),
                        pltpu.VMEM((devices * capacity * block_rows, own_rows), jnp.bfloat16),
                        pltpu.VMEM((rows, part_width), jnp.bfloat16),
                        pltpu.VMEM((4, GROUP * block_rows, own_rows), jnp.bfloat16),
                        pltpu.SemaphoreType.DMA,
                        pltpu.SemaphoreType.DMA((devices,)),
                        pltpu.SemaphoreType.DMA((4,)),
                    ],
                ),
                out_shape=jax.ShapeDtypeStruct((own_rows, part_width), jnp.float32),
                compiler_params=pltpu.CompilerParams(vmem_limit_bytes=VMEM_BYTES),
                cost_estimate=pl.CostEstimate(
                    flops=2 * requests * block_rows * own_rows * part_width,
                    bytes_accessed=slots * block_rows * own_rows * 2,
                    transcendentals=0,
                ),
                name="labels",
            )(
                step_tile, position, used, own_slot, own_place, me.reshape(1), weights, piece, factor,
                factor,
            )
        )
    return outs[0] if splits == 1 else jnp.concatenate(outs, axis=1)


def solution(mesh):
    in_specs = (P("dp", None), P("tensor"), P("dp", "tensor"), P("dp", None), P("dp"))
    out_specs = P("dp", "tensor")
    return jax.shard_map(
        on_device, mesh=mesh, in_specs=in_specs, out_specs=out_specs, check_vma=False
    )
```

```python
import functools
import math

import jax
import jax.numpy as jnp
from jax import lax
from jax.experimental import pallas as pl
from jax.experimental.pallas import tpu as pltpu
from jax.sharding import PartitionSpec as P

ALPHA = 0.75
SOFTMAX_TEMPER = 0.05
EPSILON = 1e-06
GROUP = 16
VMEM_BYTES = 60 * 1024 * 1024


def unitnorm_rows(features):
    wide = features.astype(jnp.float32)
    scale = lax.rsqrt(jnp.mean(wide * wide, axis=1, keepdims=True) + EPSILON)
    return (wide * scale / math.sqrt(wide.shape[1])).astype(jnp.bfloat16)


def weights_kernel(
    block_rows, tile_rows, step_tile, slot_block, slot_first, used, counts, memory, out, factor,
    held, total, sem
):
    step = pl.program_id(0)
    rows = memory.shape[0]

    @pl.when(step == 0)
    def _():
        copy = pltpu.make_async_copy(memory, held.at[pl.ds(0, rows)], sem)
        copy.start()
        copy.wait()

    @pl.when(step < used[0])
    def _():
        tile = step_tile[step]
        starts = [
            pl.multiple_of(slot_block[step * GROUP + j] * block_rows, block_rows)
            for j in range(GROUP)
        ]
        keys = held[pl.ds(pl.multiple_of(tile * tile_rows, tile_rows), tile_rows), :]
        some = GROUP // 2
        where = [pl.ds(start, block_rows) for start in starts]
        olds = [
            jnp.where(slot_first[step * GROUP + j] == 1, 0.0, total[where[j], :])
            for j in range(GROUP)
        ]
        news = []
        for begin in range(0, GROUP, some):
            queries = jnp.concatenate(
                [held[rows_at, :] for rows_at in where[begin : begin + some]], axis=0
            )
            scores = lax.dot_general(
                queries, keys, (((1,), (1,)), ((), ())), preferred_element_type=jnp.float32
            )
            columns = lax.broadcasted_iota(jnp.int32, scores.shape, 1)
            weights = jnp.where(
                columns < counts[tile], jnp.exp(scores * (1.0 / SOFTMAX_TEMPER)), 0.0
            ).astype(jnp.bfloat16)
            out[begin * block_rows : (begin + some) * block_rows, :] = weights
            sums = jnp.sum(weights.astype(jnp.float32), axis=1, keepdims=True)
            for j in range(some):
                news.append(olds[begin + j] + sums[j * block_rows : (j + 1) * block_rows])
        for j in range(GROUP):
            total[where[j], :] = news[j]

    @pl.when(step == pl.num_programs(0) - 1)
    def _():
        factor[...] = ALPHA / total[pl.ds(0, rows), :]


def labels_kernel(
    chunks, block_rows, own_slots, step_tile, position, used, own_slot, own_place, me,
    all_weights, all_priors, factor, own_factor, out, partial, own_partial, own_weights, prior,
    ring, sem, prior_sems, ring_sems
):
    step = pl.program_id(0)
    tile_rows, width = out.shape
    tiles = prior.shape[0] // tile_rows
    size = ring.shape[1]
    depth = ring.shape[0]
    tile_blocks = tile_rows // block_rows
    piece = 256 if width % 256 == 0 else 128
    pieces = [slice(p, p + piece) for p in range(0, width, piece)]

    def summed(source, places, base, cut):
        found = []
        for j in range(tile_blocks):
            pair = [
                source[pl.ds(pl.multiple_of(places[base + 2 * j + k] * block_rows, block_rows),
                             block_rows), cut].astype(jnp.float32)
                for k in range(2)
            ]
            found.append(pair[0] + pair[1])
        return jnp.concatenate(found, axis=0)

    def wide(lanes):
        return jnp.concatenate([lanes] * (piece // 128), axis=1)

    def prior_rows(tile):
        return pl.ds(pl.multiple_of(tile * tile_rows, tile_rows), tile_rows)

    def prior_copy(tile):
        return pltpu.make_async_copy(
            all_priors.at[prior_rows(tile)], prior.at[prior_rows(tile)], prior_sems.at[tile]
        )

    def ring_copy(chunk):
        return pltpu.make_async_copy(
            all_weights.at[pl.ds(pl.multiple_of(chunk * size, size), size)],
            ring.at[chunk % depth],
            ring_sems.at[chunk % depth],
        )

    def fetch(chunk):
        @pl.when(chunk < used[0])
        def _():
            ring_copy(chunk).start()

    @pl.when(step == 0)
    def _():
        fetch(0)

        @pl.loop(0, tiles)
        def _(tile):
            prior_copy(tile).start()

        for chunk in range(1, depth - 1):
            fetch(chunk)

        @pl.loop(0, own_weights.shape[0] // block_rows)
        def _(i):
            start = pl.multiple_of(own_slot[i] * block_rows, block_rows)
            pltpu.make_async_copy(
                all_weights.at[pl.ds(start, block_rows)],
                own_weights.at[pl.ds(pl.multiple_of(i * block_rows, block_rows), block_rows)],
                sem,
            ).start()

    before = jnp.where(step == 0, -1, step_tile[jnp.maximum(step - 1, 0)])

    @pl.when(step == chunks)
    def _():
        pltpu.make_async_copy(
            all_weights.at[pl.ds(0, own_weights.shape[0])], own_weights, sem
        ).wait()

        @pl.loop(before + 1, tiles)
        def _(tile):
            prior_copy(tile).wait()

    @pl.when(step < used[0])
    def _():
        fetch(step + depth - 1)

        @pl.loop(before + 1, step_tile[step] + 1)
        def _(tile):
            prior_copy(tile).wait()

        ring_copy(step).wait()
        rows = pl.ds(pl.multiple_of(step * size, size), size)
        weights = ring[step % depth]
        for cut in pieces:
            part = jnp.dot(
                weights, prior[prior_rows(step_tile[step]), cut],
                preferred_element_type=jnp.float32,
            )
            partial[rows, cut] = part.astype(jnp.bfloat16)

    @pl.when(step >= chunks)
    def _():
        tile = step - chunks
        count = own_slots * block_rows
        rows = pl.ds(pl.multiple_of(tile * count, count), count)
        sent = own_weights[rows, :]
        scale = wide(factor[...])
        for cut in pieces:
            numerator = summed(partial, position, tile * tile_blocks * 2, cut)
            labels = numerator * scale
            labels += (1.0 - ALPHA) * prior[prior_rows(tile), cut].astype(jnp.float32)
            part = jnp.dot(
                sent, labels.astype(jnp.bfloat16), preferred_element_type=jnp.float32
            )
            own_partial[rows, cut] = part.astype(jnp.bfloat16)

    @pl.when(step == pl.num_programs(0) - 1)
    def _():
        scale = wide(own_factor[...])
        for cut in pieces:
            spread = summed(own_partial, own_place, 0, cut) * scale
            spread += (1.0 - ALPHA) * prior[prior_rows(me[0]), cut].astype(jnp.float32)
            out[:, cut] = jnp.log(spread)


def gather_kernel(
    features, logits, bias, lists, memory, priors, all_lists, labels, raised, sums, twin_sums,
    recv, send, local, sums_sent, sums_came
):
    dp, y = lax.axis_index("dp"), lax.axis_index("tensor")
    z, x, c = dp // 4, (dp // 2) % 2, dp % 2
    rows = features.shape[0]
    half = rows // 2

    def index(zz, xx):
        return zz * 4 + xx * 2 + c

    def region(t, kind):
        if kind == 3:
            return all_lists.at[t]
        if kind == 2:
            return priors.at[pl.ds(pl.multiple_of(t * rows, rows), rows)]
        h = y if kind == 0 else 1 - y
        return memory.at[pl.ds(pl.multiple_of(t * rows + h * half, half), half)]

    def own_region(kind):
        if kind == 3:
            return lists
        if kind == 2:
            return labels
        h = y if kind == 0 else 1 - y
        return features.at[pl.ds(pl.multiple_of(h * half, half), half)]

    def partner(way):
        if way == 0:
            return {"dp": dp - 4}
        if way == 1:
            return {"dp": dp + 4}
        if way == 2:
            return {"dp": dp + 2 - 4 * x}
        if way == 3:
            return {"tensor": 1 - y}
        return {"dp": dp + 1 - 2 * c}

    def reach(way):
        if way == 0:
            return z > 0
        if way == 1:
            return z < 3
        return None

    def guarded(conditions, body):
        conditions = [q for q in conditions if q is not None]
        if not conditions:
            body()
        else:
            both = conditions[0]
            for q in conditions[1:]:
                both = jnp.logical_and(both, q)
            pl.when(both)(body)

    sent = []

    def copy(zz, xx, kind, way, own):
        t = index(zz, xx)
        arrives = 1 if way == 3 else kind
        return pltpu.make_async_remote_copy(
            src_ref=own_region(kind) if own else region(t, kind),
            dst_ref=region(t, kind),
            send_sem=send.at[zz * 2 + xx, kind, way],
            recv_sem=recv.at[t, arrives],
            device_id=partner(way),
            device_id_type=pl.DeviceIdType.MESH,
        )

    def push(zz, xx, kind, ways, exists=None, own=False, skip_across=None):
        for way in ways:
            guards = (exists, reach(way), skip_across if way == 2 else None)
            guarded(guards, lambda way=way: copy(zz, xx, kind, way, own).start())
            sent.append((guards, zz, xx, kind, way, own))

    def landed(t, kind):
        pltpu.make_async_remote_copy(
            src_ref=region(t, kind), dst_ref=region(t, kind),
            send_sem=send.at[0, 0, 0], recv_sem=recv.at[t, kind],
            device_id=partner(4), device_id_type=pl.DeviceIdType.MESH,
        ).wait_recv()

    def column(distance):
        if distance == 0:
            return [(z, None, (0, 1))]
        return [
            (z - distance, z >= distance, (1,)),
            (z + distance, z + distance < 4, (0,)),
        ]

    def near(distance, kind):
        for zz, exists, ways in column(distance):
            guarded((exists,), lambda zz=zz: landed(index(zz, x), kind))
            onward = ways + ((2, 3, 4) if kind == 0 else (2, 4))
            paired = zz != z + 1 - 2 * (z % 2) if kind == 2 and distance == 1 else None
            push(zz, x, kind, onward, exists, skip_across=paired)

    def across(distance, kind):
        for zz, exists, _ in column(distance):
            guarded((exists,), lambda zz=zz: landed(index(zz, 1 - x), kind))
            push(zz, 1 - x, kind, (3, 4) if kind == 0 else (4,), exists)
            if kind == 2 and distance == 0:
                push(zz, 1 - x, kind, (1,), z % 2 == 0)
                push(zz, 1 - x, kind, (0,), z % 2 == 1)

    def mirrored(distance, xx):
        for zz, exists, _ in column(distance):
            guarded((exists,), lambda zz=zz: landed(index(zz, xx), 1))
            push(zz, xx, 1, (4,), exists)

    barrier = pltpu.get_barrier_semaphore()
    for way in range(5):
        guarded(
            (reach(way),),
            lambda way=way: pl.semaphore_signal(
                barrier, inc=1, device_id=partner(way), device_id_type=pl.DeviceIdType.MESH
            ),
        )
    pl.semaphore_wait(barrier, 4 + z * (3 - z) // 2)

    push(z, x, 0, (0, 1, 2, 4), own=True)
    push(z, x, 3, (0, 1, 2, 4), own=True)
    keep = pl.ds(pl.multiple_of(dp * rows, rows), rows)
    copies = [
        pltpu.make_async_copy(features, memory.at[keep], local.at[0]),
        pltpu.make_async_copy(lists, all_lists.at[dp], local.at[1]),
        pltpu.make_async_copy(labels, priors.at[keep], local.at[2]),
    ]
    for one in copies[:2]:
        one.start()
    slab = 64

    @pl.loop(0, rows // slab)
    def _(i):
        at = pl.ds(pl.multiple_of(i * slab, slab), slab)
        grown = jnp.exp(logits[at, :].astype(jnp.float32) + bias[...])
        raised[at, :] = grown
        sums[at, :] = jnp.broadcast_to(jnp.sum(grown, axis=1, keepdims=True), (slab, 128))

    swap = pltpu.make_async_remote_copy(
        src_ref=sums, dst_ref=twin_sums, send_sem=sums_sent, recv_sem=sums_came,
        device_id=partner(3), device_id_type=pl.DeviceIdType.MESH,
    )
    swap.start()
    swap.wait()

    @pl.loop(0, rows // slab)
    def _(i):
        at = pl.ds(pl.multiple_of(i * slab, slab), slab)
        whole = sums[at, :] + twin_sums[at, :]
        whole = jnp.concatenate([whole] * (raised.shape[1] // 128), axis=1)
        labels[at, :] = (raised[at, :] / whole).astype(jnp.bfloat16)

    copies[2].start()
    for distance in (1, 2, 3):
        near(distance, 0)
        across(distance - 1, 0)
        near(distance, 3)
        across(distance - 1, 3)
        if distance == 2:
            push(z, x, 2, (0, 1, 2, 4), own=True)
            push(z, x, 1, (4,), own=True)
    across(3, 0)
    across(3, 3)
    for distance in (1, 2, 3):
        near(distance, 2)
        across(distance - 1, 2)
        mirrored(distance, x)
        mirrored(distance - 1, 1 - x)
    mirrored(3, 1 - x)
    across(3, 2)
    for zz in range(4):
        for xx in range(2):
            for kind in range(4):
                landed(zz * 4 + xx * 2 + 1 - c, kind)
    for guards, zz, xx, kind, way, own in sent:
        guarded(
            guards,
            lambda zz=zz, xx=xx, kind=kind, way=way, own=own: copy(
                zz, xx, kind, way, own
            ).wait_send(),
        )
    for one in copies:
        one.wait()


def gather_all(normalized, logits, bias, lists, devices):
    rows, width = normalized.shape
    classes = logits.shape[1]
    return pl.pallas_call(
        gather_kernel,
        in_specs=[
            pl.BlockSpec(memory_space=pl.ANY),
            pl.BlockSpec(memory_space=pltpu.VMEM),
            pl.BlockSpec(memory_space=pltpu.VMEM),
            pl.BlockSpec(memory_space=pl.ANY),
        ],
        out_specs=[pl.BlockSpec(memory_space=pl.ANY)] * 3,
        out_shape=[
            jax.ShapeDtypeStruct((devices * rows, width), normalized.dtype),
            jax.ShapeDtypeStruct((devices * rows, classes), jnp.bfloat16),
            jax.ShapeDtypeStruct((devices,) + lists.shape, lists.dtype),
        ],
        scratch_shapes=[
            pltpu.VMEM((rows, classes), jnp.bfloat16),
            pltpu.VMEM((rows, classes), jnp.float32),
            pltpu.VMEM((rows, 128), jnp.float32),
            pltpu.VMEM((rows, 128), jnp.float32),
            pltpu.SemaphoreType.DMA((devices, 4)),
            pltpu.SemaphoreType.DMA((8, 4, 5)),
            pltpu.SemaphoreType.DMA((3,)),
            pltpu.SemaphoreType.DMA,
            pltpu.SemaphoreType.DMA,
        ],
        compiler_params=pltpu.CompilerParams(
            collective_id=0, has_side_effects=True, vmem_limit_bytes=VMEM_BYTES
        ),
        cost_estimate=pl.CostEstimate(
            flops=0, bytes_accessed=2 * devices * rows * (width + classes) * 2, transcendentals=0
        ),
        name="gather",
    )(normalized, logits, bias, lists)


def on_device(features, class_bias, logits, tile_lists, valid_counts):
    devices = lax.axis_size("dp")
    twins = lax.axis_size("tensor")
    own_rows, width = features.shape
    block_count, listed = tile_lists.shape
    block_rows = own_rows // block_count
    rows = own_rows * devices
    blocks = block_count * devices
    requests = blocks * listed
    chunks = (requests + devices * (GROUP - 1)) // GROUP
    slots = chunks * GROUP
    me = lax.axis_index("dp").astype(jnp.int32)
    twin = lax.axis_index("tensor")

    normalized = unitnorm_rows(features)
    grid_links = devices == 16 and twins == 2
    splits = 1 if grid_links else 2
    part_width = logits.shape[1] // splits
    small = jnp.concatenate([tile_lists.reshape(-1), valid_counts])
    listing = small.shape[0]
    if grid_links:
        lists = jnp.pad(small, (0, 8 * 128 - listing)).reshape(8, 128)
        memory, gathered, all_lists = gather_all(
            normalized, logits, class_bias[None, :], lists, devices
        )
        priors = [gathered]
        small = all_lists.reshape(devices, -1)[:, :listing]
    else:
        adjusted = logits.astype(jnp.float32) + class_bias[None, :]
        exponentials = jnp.exp(adjusted)
        row_totals = lax.psum(jnp.sum(exponentials, axis=1), "tensor")
        prior = (exponentials / row_totals[:, None]).astype(jnp.bfloat16)
        own_priors = [prior[:, s * part_width : (s + 1) * part_width] for s in range(splits)]
        share = own_rows // twins
        mine = lax.dynamic_slice_in_dim(normalized, twin * share, share, 0)
        memory = lax.all_gather(mine, ("dp", "tensor"), axis=0, tiled=True)
        small = lax.all_gather(small, "dp", axis=0, tiled=False)
        priors = [lax.all_gather(p, "dp", axis=0, tiled=True) for p in own_priors]
    counts = small[:, -1]
    owners = small[:, :-1].reshape(-1)
    pairs = owners.reshape(-1, listed)
    firsts = jnp.stack([pairs[:, 0] < pairs[:, 1], pairs[:, 1] < pairs[:, 0]], axis=1)
    firsts = firsts.reshape(-1).astype(jnp.int32)
    hits = (owners[:, None] == jnp.arange(devices, dtype=jnp.int32)[None, :]).astype(jnp.int32)
    running = jnp.cumsum(hits, axis=0)
    earlier = jnp.sum((running - hits) * hits, axis=1)
    tile_chunks = (running[-1] + GROUP - 1) // GROUP
    ends = jnp.cumsum(tile_chunks)
    bases = ends - tile_chunks
    position = jnp.sum(hits * bases[None, :], axis=1) * GROUP + earlier
    matches = position[None, :] == jnp.arange(slots, dtype=jnp.int32)[:, None]
    request_ids = jnp.arange(requests, dtype=jnp.int32)
    filled = jnp.any(matches, axis=1)
    source = jnp.sum(jnp.where(matches, request_ids[None, :], 0), axis=1)
    slot_block = jnp.where(filled, source // listed, blocks)
    slot_first = jnp.sum(jnp.where(matches, firsts[None, :], 0), axis=1)
    used = ends[-1:]
    steps = jnp.minimum(jnp.arange(chunks, dtype=jnp.int32), used[0] - 1)
    chunk_tile = jnp.sum((steps[:, None] >= ends[None, :]).astype(jnp.int32), axis=1)
    step_tile = jnp.concatenate([chunk_tile, jnp.arange(devices, dtype=jnp.int32)])

    capacity = max(2, 64 // devices)
    own_requests = block_count * listed
    own_owners = tile_lists.reshape(-1)
    own_hits = (own_owners[:, None] == jnp.arange(devices, dtype=jnp.int32)[None, :]).astype(
        jnp.int32
    )
    own_earlier = jnp.sum((jnp.cumsum(own_hits, axis=0) - own_hits) * own_hits, axis=1)
    own_place = own_owners * capacity + own_earlier
    own_matches = (
        own_place[None, :] == jnp.arange(devices * capacity, dtype=jnp.int32)[:, None]
    )

    def placed(values):
        return jnp.sum(jnp.where(own_matches, values[None, :], 0), axis=1)

    own_slot = placed(lax.dynamic_slice_in_dim(position, me * own_requests, own_requests))

    def one_chunk(step, tiles, sb, sf, n, *rest):
        return (jnp.minimum(step, n[0] - 1), 0)

    weights, factor = pl.pallas_call(
        functools.partial(weights_kernel, block_rows, own_rows),
        grid_spec=pltpu.PrefetchScalarGridSpec(
            num_scalar_prefetch=5,
            grid=(chunks,),
            in_specs=[pl.BlockSpec(memory_space=pl.ANY)],
            out_specs=[
                pl.BlockSpec((GROUP * block_rows, own_rows), one_chunk),
                pl.BlockSpec((rows, 128), lambda *a: (0, 0), pipeline_mode=pl.Buffered(1)),
            ],
            scratch_shapes=[
                pltpu.VMEM((rows + block_rows, width), jnp.bfloat16),
                pltpu.VMEM((rows + block_rows, 128), jnp.float32),
                pltpu.SemaphoreType.DMA,
            ],
        ),
        out_shape=[
            jax.ShapeDtypeStruct((slots * block_rows, own_rows), jnp.bfloat16),
            jax.ShapeDtypeStruct((rows, 128), jnp.float32),
        ],
        compiler_params=pltpu.CompilerParams(vmem_limit_bytes=VMEM_BYTES),
        cost_estimate=pl.CostEstimate(
            flops=2 * requests * block_rows * own_rows * width,
            bytes_accessed=rows * width * 2 + slots * block_rows * own_rows * 2,
            transcendentals=requests * block_rows * own_rows,
        ),
        name="weights",
    )(step_tile, slot_block, slot_first, used, counts, memory)

    def late_tile(step, *rest):
        return (jnp.maximum(step - chunks, 0), 0)

    def same(*a):
        return (0, 0)

    def mine_at(step, tiles, ps, n, os, op, m):
        return (m[0], 0)

    outs = []
    for piece in priors:
        outs.append(
            pl.pallas_call(
                functools.partial(labels_kernel, chunks, block_rows, capacity),
                grid_spec=pltpu.PrefetchScalarGridSpec(
                    num_scalar_prefetch=6,
                    grid=(chunks + devices,),
                    in_specs=[
                        pl.BlockSpec(memory_space=pl.ANY),
                        pl.BlockSpec(memory_space=pl.ANY),
                        pl.BlockSpec((own_rows, 128), late_tile),
                        pl.BlockSpec(
                            (own_rows, 128), mine_at, pipeline_mode=pl.Buffered(1)
                        ),
                    ],
                    out_specs=pl.BlockSpec(
                        (own_rows, part_width), same, pipeline_mode=pl.Buffered(1)
                    ),
                    scratch_shapes=[
                        pltpu.VMEM((slots * block_rows, part_width), jnp.bfloat16),
                        pltpu.VMEM(
                            (devices * capacity * block_rows, part_width), jnp.bfloat16
                        ),
                        pltpu.VMEM((devices * capacity * block_rows, own_rows), jnp.bfloat16),
                        pltpu.VMEM((rows, part_width), jnp.bfloat16),
                        pltpu.VMEM((4, GROUP * block_rows, own_rows), jnp.bfloat16),
                        pltpu.SemaphoreType.DMA,
                        pltpu.SemaphoreType.DMA((devices,)),
                        pltpu.SemaphoreType.DMA((4,)),
                    ],
                ),
                out_shape=jax.ShapeDtypeStruct((own_rows, part_width), jnp.float32),
                compiler_params=pltpu.CompilerParams(vmem_limit_bytes=VMEM_BYTES),
                cost_estimate=pl.CostEstimate(
                    flops=2 * requests * block_rows * own_rows * part_width,
                    bytes_accessed=slots * block_rows * own_rows * 2,
                    transcendentals=0,
                ),
                name="labels",
            )(
                step_tile, position, used, own_slot, own_place, me.reshape(1), weights, piece, factor,
                factor,
            )
        )
    return outs[0] if splits == 1 else jnp.concatenate(outs, axis=1)


def solution(mesh):
    in_specs = (P("dp", None), P("tensor"), P("dp", "tensor"), P("dp", None), P("dp"))
    out_specs = P("dp", "tensor")
    return jax.shard_map(
        on_device, mesh=mesh, in_specs=in_specs, out_specs=out_specs, check_vma=False
    )
```

```python
import functools
import math

import jax
import jax.numpy as jnp
from jax import lax
from jax.experimental import pallas as pl
from jax.experimental.pallas import tpu as pltpu
from jax.sharding import PartitionSpec as P

ALPHA = 0.75
SOFTMAX_TEMPER = 0.05
EPSILON = 1e-06
GROUP = 16
VMEM_BYTES = 60 * 1024 * 1024


def unitnorm_rows(features):
    wide = features.astype(jnp.float32)
    scale = lax.rsqrt(jnp.mean(wide * wide, axis=1, keepdims=True) + EPSILON)
    return (wide * scale / math.sqrt(wide.shape[1])).astype(jnp.bfloat16)


def weights_kernel(
    block_rows, tile_rows, step_tile, slot_block, slot_first, used, counts, memory, out, factor,
    held, total, sem
):
    step = pl.program_id(0)
    rows = memory.shape[0]

    @pl.when(step == 0)
    def _():
        copy = pltpu.make_async_copy(memory, held.at[pl.ds(0, rows)], sem)
        copy.start()
        copy.wait()

    @pl.when(step < used[0])
    def _():
        tile = step_tile[step]
        starts = [
            pl.multiple_of(slot_block[step * GROUP + j] * block_rows, block_rows)
            for j in range(GROUP)
        ]
        keys = held[pl.ds(pl.multiple_of(tile * tile_rows, tile_rows), tile_rows), :]
        some = GROUP // 2
        where = [pl.ds(start, block_rows) for start in starts]
        olds = [
            jnp.where(slot_first[step * GROUP + j] == 1, 0.0, total[where[j], :])
            for j in range(GROUP)
        ]
        news = []
        for begin in range(0, GROUP, some):
            queries = jnp.concatenate(
                [held[rows_at, :] for rows_at in where[begin : begin + some]], axis=0
            )
            scores = lax.dot_general(
                queries, keys, (((1,), (1,)), ((), ())), preferred_element_type=jnp.float32
            )
            columns = lax.broadcasted_iota(jnp.int32, scores.shape, 1)
            weights = jnp.where(
                columns < counts[tile], jnp.exp(scores * (1.0 / SOFTMAX_TEMPER)), 0.0
            ).astype(jnp.bfloat16)
            out[begin * block_rows : (begin + some) * block_rows, :] = weights
            sums = jnp.sum(weights.astype(jnp.float32), axis=1, keepdims=True)
            for j in range(some):
                news.append(olds[begin + j] + sums[j * block_rows : (j + 1) * block_rows])
        for j in range(GROUP):
            total[where[j], :] = news[j]

    @pl.when(step == pl.num_programs(0) - 1)
    def _():
        factor[...] = ALPHA / total[pl.ds(0, rows), :]


def labels_kernel(
    chunks, block_rows, own_slots, step_tile, position, used, own_slot, own_place, me,
    all_weights, all_priors, factor, own_factor, out, partial, own_partial, own_weights, prior,
    ring, sem, prior_sems, ring_sems
):
    step = pl.program_id(0)
    tile_rows, width = out.shape
    tiles = prior.shape[0] // tile_rows
    size = ring.shape[1]
    depth = ring.shape[0]
    tile_blocks = tile_rows // block_rows
    piece = 256 if width % 256 == 0 else 128
    pieces = [slice(p, p + piece) for p in range(0, width, piece)]

    def summed(source, places, base, cut):
        found = []
        for j in range(tile_blocks):
            pair = [
                source[pl.ds(pl.multiple_of(places[base + 2 * j + k] * block_rows, block_rows),
                             block_rows), cut].astype(jnp.float32)
                for k in range(2)
            ]
            found.append(pair[0] + pair[1])
        return jnp.concatenate(found, axis=0)

    def wide(lanes):
        return jnp.concatenate([lanes] * (piece // 128), axis=1)

    def prior_rows(tile):
        return pl.ds(pl.multiple_of(tile * tile_rows, tile_rows), tile_rows)

    def prior_copy(tile):
        return pltpu.make_async_copy(
            all_priors.at[prior_rows(tile)], prior.at[prior_rows(tile)], prior_sems.at[tile]
        )

    def ring_copy(chunk):
        return pltpu.make_async_copy(
            all_weights.at[pl.ds(pl.multiple_of(chunk * size, size), size)],
            ring.at[chunk % depth],
            ring_sems.at[chunk % depth],
        )

    def fetch(chunk):
        @pl.when(chunk < used[0])
        def _():
            ring_copy(chunk).start()

    @pl.when(step == 0)
    def _():
        fetch(0)

        @pl.loop(0, tiles)
        def _(tile):
            prior_copy(tile).start()

        for chunk in range(1, depth - 1):
            fetch(chunk)

        @pl.loop(0, own_weights.shape[0] // block_rows)
        def _(i):
            start = pl.multiple_of(own_slot[i] * block_rows, block_rows)
            pltpu.make_async_copy(
                all_weights.at[pl.ds(start, block_rows)],
                own_weights.at[pl.ds(pl.multiple_of(i * block_rows, block_rows), block_rows)],
                sem,
            ).start()

    before = jnp.where(step == 0, -1, step_tile[jnp.maximum(step - 1, 0)])

    @pl.when(step == chunks)
    def _():
        pltpu.make_async_copy(
            all_weights.at[pl.ds(0, own_weights.shape[0])], own_weights, sem
        ).wait()

        @pl.loop(before + 1, tiles)
        def _(tile):
            prior_copy(tile).wait()

    @pl.when(step < used[0])
    def _():
        fetch(step + depth - 1)

        @pl.loop(before + 1, step_tile[step] + 1)
        def _(tile):
            prior_copy(tile).wait()

        ring_copy(step).wait()
        rows = pl.ds(pl.multiple_of(step * size, size), size)
        weights = ring[step % depth]
        for cut in pieces:
            part = jnp.dot(
                weights, prior[prior_rows(step_tile[step]), cut],
                preferred_element_type=jnp.float32,
            )
            partial[rows, cut] = part.astype(jnp.bfloat16)

    @pl.when(step >= chunks)
    def _():
        tile = step - chunks
        count = own_slots * block_rows
        rows = pl.ds(pl.multiple_of(tile * count, count), count)
        sent = own_weights[rows, :]
        scale = wide(factor[...])
        for cut in pieces:
            numerator = summed(partial, position, tile * tile_blocks * 2, cut)
            labels = numerator * scale
            labels += (1.0 - ALPHA) * prior[prior_rows(tile), cut].astype(jnp.float32)
            part = jnp.dot(
                sent, labels.astype(jnp.bfloat16), preferred_element_type=jnp.float32
            )
            own_partial[rows, cut] = part.astype(jnp.bfloat16)

    @pl.when(step == pl.num_programs(0) - 1)
    def _():
        scale = wide(own_factor[...])
        for cut in pieces:
            spread = summed(own_partial, own_place, 0, cut) * scale
            spread += (1.0 - ALPHA) * prior[prior_rows(me[0]), cut].astype(jnp.float32)
            out[:, cut] = jnp.log(spread)


def gather_kernel(
    features, logits, bias, lists, memory, priors, all_lists, labels, raised, sums, twin_sums,
    recv, send, local, sums_sent, sums_came
):
    dp, y = lax.axis_index("dp"), lax.axis_index("tensor")
    z, x, c = dp // 4, (dp // 2) % 2, dp % 2
    rows = features.shape[0]
    half = rows // 2

    def index(zz, xx):
        return zz * 4 + xx * 2 + c

    def region(t, kind):
        if kind == 3:
            return all_lists.at[t]
        if kind == 2:
            return priors.at[pl.ds(pl.multiple_of(t * rows, rows), rows)]
        h = y if kind == 0 else 1 - y
        return memory.at[pl.ds(pl.multiple_of(t * rows + h * half, half), half)]

    def own_region(kind):
        if kind == 3:
            return lists
        if kind == 2:
            return labels
        h = y if kind == 0 else 1 - y
        return features.at[pl.ds(pl.multiple_of(h * half, half), half)]

    def partner(way):
        if way == 0:
            return {"dp": dp - 4}
        if way == 1:
            return {"dp": dp + 4}
        if way == 2:
            return {"dp": dp + 2 - 4 * x}
        if way == 3:
            return {"tensor": 1 - y}
        return {"dp": dp + 1 - 2 * c}

    def reach(way):
        if way == 0:
            return z > 0
        if way == 1:
            return z < 3
        return None

    def guarded(conditions, body):
        conditions = [q for q in conditions if q is not None]
        if not conditions:
            body()
        else:
            both = conditions[0]
            for q in conditions[1:]:
                both = jnp.logical_and(both, q)
            pl.when(both)(body)

    sent = []

    def copy(zz, xx, kind, way, own):
        t = index(zz, xx)
        arrives = 1 if way == 3 else kind
        return pltpu.make_async_remote_copy(
            src_ref=own_region(kind) if own else region(t, kind),
            dst_ref=region(t, kind),
            send_sem=send.at[zz * 2 + xx, kind, way],
            recv_sem=recv.at[t, arrives],
            device_id=partner(way),
            device_id_type=pl.DeviceIdType.MESH,
        )

    def push(zz, xx, kind, ways, exists=None, own=False, skip_across=None):
        for way in ways:
            guards = (exists, reach(way), skip_across if way == 2 else None)
            guarded(guards, lambda way=way: copy(zz, xx, kind, way, own).start())
            sent.append((guards, zz, xx, kind, way, own))

    def landed(t, kind):
        pltpu.make_async_remote_copy(
            src_ref=region(t, kind), dst_ref=region(t, kind),
            send_sem=send.at[0, 0, 0], recv_sem=recv.at[t, kind],
            device_id=partner(4), device_id_type=pl.DeviceIdType.MESH,
        ).wait_recv()

    def column(distance):
        if distance == 0:
            return [(z, None, (0, 1))]
        return [
            (z - distance, z >= distance, (1,)),
            (z + distance, z + distance < 4, (0,)),
        ]

    def near(distance, kind):
        for zz, exists, ways in column(distance):
            guarded((exists,), lambda zz=zz: landed(index(zz, x), kind))
            onward = ways + ((2, 3, 4) if kind == 0 else (2, 4))
            paired = None
            if kind == 2 and distance == 1:
                paired = jnp.logical_or(zz != z + 1 - 2 * (z % 2), z % 3 == 0)
            push(zz, x, kind, onward, exists, skip_across=paired)

    def across(distance, kind):
        for zz, exists, _ in column(distance):
            guarded((exists,), lambda zz=zz: landed(index(zz, 1 - x), kind))
            push(zz, 1 - x, kind, (3, 4) if kind == 0 else (4,), exists)
            if kind == 2 and distance == 0:
                push(zz, 1 - x, kind, (1,), z == 0)
                push(zz, 1 - x, kind, (0,), z == 3)

    def mirrored(distance, xx):
        for zz, exists, _ in column(distance):
            guarded((exists,), lambda zz=zz: landed(index(zz, xx), 1))
            push(zz, xx, 1, (4,), exists)

    barrier = pltpu.get_barrier_semaphore()
    for way in range(5):
        guarded(
            (reach(way),),
            lambda way=way: pl.semaphore_signal(
                barrier, inc=1, device_id=partner(way), device_id_type=pl.DeviceIdType.MESH
            ),
        )
    pl.semaphore_wait(barrier, 4 + z * (3 - z) // 2)

    push(z, x, 0, (0, 1, 2, 4), own=True)
    push(z, x, 3, (0, 1, 2, 4), own=True)
    keep = pl.ds(pl.multiple_of(dp * rows, rows), rows)
    copies = [
        pltpu.make_async_copy(features, memory.at[keep], local.at[0]),
        pltpu.make_async_copy(lists, all_lists.at[dp], local.at[1]),
        pltpu.make_async_copy(labels, priors.at[keep], local.at[2]),
    ]
    for one in copies[:2]:
        one.start()
    slab = 64

    @pl.loop(0, rows // slab)
    def _(i):
        at = pl.ds(pl.multiple_of(i * slab, slab), slab)
        grown = jnp.exp(logits[at, :].astype(jnp.float32) + bias[...])
        raised[at, :] = grown
        sums[at, :] = jnp.broadcast_to(jnp.sum(grown, axis=1, keepdims=True), (slab, 128))

    swap = pltpu.make_async_remote_copy(
        src_ref=sums, dst_ref=twin_sums, send_sem=sums_sent, recv_sem=sums_came,
        device_id=partner(3), device_id_type=pl.DeviceIdType.MESH,
    )
    swap.start()
    swap.wait()

    @pl.loop(0, rows // slab)
    def _(i):
        at = pl.ds(pl.multiple_of(i * slab, slab), slab)
        whole = sums[at, :] + twin_sums[at, :]
        whole = jnp.concatenate([whole] * (raised.shape[1] // 128), axis=1)
        labels[at, :] = (raised[at, :] / whole).astype(jnp.bfloat16)

    copies[2].start()
    for distance in (1, 2, 3):
        near(distance, 0)
        across(distance - 1, 0)
        near(distance, 3)
        across(distance - 1, 3)
        if distance == 1:
            push(z, x, 2, (0, 1, 2, 4), own=True)
            push(z, x, 1, (4,), own=True)
    across(3, 0)
    across(3, 3)
    for distance in (1, 2, 3):
        near(distance, 2)
        across(distance - 1, 2)
        mirrored(distance, x)
        mirrored(distance - 1, 1 - x)
    mirrored(3, 1 - x)
    across(3, 2)
    for zz in range(4):
        for xx in range(2):
            for kind in range(4):
                landed(zz * 4 + xx * 2 + 1 - c, kind)
    for guards, zz, xx, kind, way, own in sent:
        guarded(
            guards,
            lambda zz=zz, xx=xx, kind=kind, way=way, own=own: copy(
                zz, xx, kind, way, own
            ).wait_send(),
        )
    for one in copies:
        one.wait()


def gather_all(normalized, logits, bias, lists, devices):
    rows, width = normalized.shape
    classes = logits.shape[1]
    return pl.pallas_call(
        gather_kernel,
        in_specs=[
            pl.BlockSpec(memory_space=pl.ANY),
            pl.BlockSpec(memory_space=pltpu.VMEM),
            pl.BlockSpec(memory_space=pltpu.VMEM),
            pl.BlockSpec(memory_space=pl.ANY),
        ],
        out_specs=[pl.BlockSpec(memory_space=pl.ANY)] * 3,
        out_shape=[
            jax.ShapeDtypeStruct((devices * rows, width), normalized.dtype),
            jax.ShapeDtypeStruct((devices * rows, classes), jnp.bfloat16),
            jax.ShapeDtypeStruct((devices,) + lists.shape, lists.dtype),
        ],
        scratch_shapes=[
            pltpu.VMEM((rows, classes), jnp.bfloat16),
            pltpu.VMEM((rows, classes), jnp.float32),
            pltpu.VMEM((rows, 128), jnp.float32),
            pltpu.VMEM((rows, 128), jnp.float32),
            pltpu.SemaphoreType.DMA((devices, 4)),
            pltpu.SemaphoreType.DMA((8, 4, 5)),
            pltpu.SemaphoreType.DMA((3,)),
            pltpu.SemaphoreType.DMA,
            pltpu.SemaphoreType.DMA,
        ],
        compiler_params=pltpu.CompilerParams(
            collective_id=0, has_side_effects=True, vmem_limit_bytes=VMEM_BYTES
        ),
        cost_estimate=pl.CostEstimate(
            flops=0, bytes_accessed=2 * devices * rows * (width + classes) * 2, transcendentals=0
        ),
        name="gather",
    )(normalized, logits, bias, lists)


def on_device(features, class_bias, logits, tile_lists, valid_counts):
    devices = lax.axis_size("dp")
    twins = lax.axis_size("tensor")
    own_rows, width = features.shape
    block_count, listed = tile_lists.shape
    block_rows = own_rows // block_count
    rows = own_rows * devices
    blocks = block_count * devices
    requests = blocks * listed
    chunks = (requests + devices * (GROUP - 1)) // GROUP
    slots = chunks * GROUP
    me = lax.axis_index("dp").astype(jnp.int32)
    twin = lax.axis_index("tensor")

    normalized = unitnorm_rows(features)
    grid_links = devices == 16 and twins == 2
    splits = 1 if grid_links else 2
    part_width = logits.shape[1] // splits
    small = jnp.concatenate([tile_lists.reshape(-1), valid_counts])
    listing = small.shape[0]
    if grid_links:
        lists = jnp.pad(small, (0, 8 * 128 - listing)).reshape(8, 128)
        memory, gathered, all_lists = gather_all(
            normalized, logits, class_bias[None, :], lists, devices
        )
        priors = [gathered]
        small = all_lists.reshape(devices, -1)[:, :listing]
    else:
        adjusted = logits.astype(jnp.float32) + class_bias[None, :]
        exponentials = jnp.exp(adjusted)
        row_totals = lax.psum(jnp.sum(exponentials, axis=1), "tensor")
        prior = (exponentials / row_totals[:, None]).astype(jnp.bfloat16)
        own_priors = [prior[:, s * part_width : (s + 1) * part_width] for s in range(splits)]
        share = own_rows // twins
        mine = lax.dynamic_slice_in_dim(normalized, twin * share, share, 0)
        memory = lax.all_gather(mine, ("dp", "tensor"), axis=0, tiled=True)
        small = lax.all_gather(small, "dp", axis=0, tiled=False)
        priors = [lax.all_gather(p, "dp", axis=0, tiled=True) for p in own_priors]
    counts = small[:, -1]
    owners = small[:, :-1].reshape(-1)
    pairs = owners.reshape(-1, listed)
    firsts = jnp.stack([pairs[:, 0] < pairs[:, 1], pairs[:, 1] < pairs[:, 0]], axis=1)
    firsts = firsts.reshape(-1).astype(jnp.int32)
    hits = (owners[:, None] == jnp.arange(devices, dtype=jnp.int32)[None, :]).astype(jnp.int32)
    running = jnp.cumsum(hits, axis=0)
    earlier = jnp.sum((running - hits) * hits, axis=1)
    tile_chunks = (running[-1] + GROUP - 1) // GROUP
    ends = jnp.cumsum(tile_chunks)
    bases = ends - tile_chunks
    position = jnp.sum(hits * bases[None, :], axis=1) * GROUP + earlier
    matches = position[None, :] == jnp.arange(slots, dtype=jnp.int32)[:, None]
    request_ids = jnp.arange(requests, dtype=jnp.int32)
    filled = jnp.any(matches, axis=1)
    source = jnp.sum(jnp.where(matches, request_ids[None, :], 0), axis=1)
    slot_block = jnp.where(filled, source // listed, blocks)
    slot_first = jnp.sum(jnp.where(matches, firsts[None, :], 0), axis=1)
    used = ends[-1:]
    steps = jnp.minimum(jnp.arange(chunks, dtype=jnp.int32), used[0] - 1)
    chunk_tile = jnp.sum((steps[:, None] >= ends[None, :]).astype(jnp.int32), axis=1)
    step_tile = jnp.concatenate([chunk_tile, jnp.arange(devices, dtype=jnp.int32)])

    capacity = max(2, 64 // devices)
    own_requests = block_count * listed
    own_owners = tile_lists.reshape(-1)
    own_hits = (own_owners[:, None] == jnp.arange(devices, dtype=jnp.int32)[None, :]).astype(
        jnp.int32
    )
    own_earlier = jnp.sum((jnp.cumsum(own_hits, axis=0) - own_hits) * own_hits, axis=1)
    own_place = own_owners * capacity + own_earlier
    own_matches = (
        own_place[None, :] == jnp.arange(devices * capacity, dtype=jnp.int32)[:, None]
    )

    def placed(values):
        return jnp.sum(jnp.where(own_matches, values[None, :], 0), axis=1)

    own_slot = placed(lax.dynamic_slice_in_dim(position, me * own_requests, own_requests))

    def one_chunk(step, tiles, sb, sf, n, *rest):
        return (jnp.minimum(step, n[0] - 1), 0)

    weights, factor = pl.pallas_call(
        functools.partial(weights_kernel, block_rows, own_rows),
        grid_spec=pltpu.PrefetchScalarGridSpec(
            num_scalar_prefetch=5,
            grid=(chunks,),
            in_specs=[pl.BlockSpec(memory_space=pl.ANY)],
            out_specs=[
                pl.BlockSpec((GROUP * block_rows, own_rows), one_chunk),
                pl.BlockSpec((rows, 128), lambda *a: (0, 0), pipeline_mode=pl.Buffered(1)),
            ],
            scratch_shapes=[
                pltpu.VMEM((rows + block_rows, width), jnp.bfloat16),
                pltpu.VMEM((rows + block_rows, 128), jnp.float32),
                pltpu.SemaphoreType.DMA,
            ],
        ),
        out_shape=[
            jax.ShapeDtypeStruct((slots * block_rows, own_rows), jnp.bfloat16),
            jax.ShapeDtypeStruct((rows, 128), jnp.float32),
        ],
        compiler_params=pltpu.CompilerParams(vmem_limit_bytes=VMEM_BYTES),
        cost_estimate=pl.CostEstimate(
            flops=2 * requests * block_rows * own_rows * width,
            bytes_accessed=rows * width * 2 + slots * block_rows * own_rows * 2,
            transcendentals=requests * block_rows * own_rows,
        ),
        name="weights",
    )(step_tile, slot_block, slot_first, used, counts, memory)

    def late_tile(step, *rest):
        return (jnp.maximum(step - chunks, 0), 0)

    def same(*a):
        return (0, 0)

    def mine_at(step, tiles, ps, n, os, op, m):
        return (m[0], 0)

    outs = []
    for piece in priors:
        outs.append(
            pl.pallas_call(
                functools.partial(labels_kernel, chunks, block_rows, capacity),
                grid_spec=pltpu.PrefetchScalarGridSpec(
                    num_scalar_prefetch=6,
                    grid=(chunks + devices,),
                    in_specs=[
                        pl.BlockSpec(memory_space=pl.ANY),
                        pl.BlockSpec(memory_space=pl.ANY),
                        pl.BlockSpec((own_rows, 128), late_tile),
                        pl.BlockSpec(
                            (own_rows, 128), mine_at, pipeline_mode=pl.Buffered(1)
                        ),
                    ],
                    out_specs=pl.BlockSpec(
                        (own_rows, part_width), same, pipeline_mode=pl.Buffered(1)
                    ),
                    scratch_shapes=[
                        pltpu.VMEM((slots * block_rows, part_width), jnp.bfloat16),
                        pltpu.VMEM(
                            (devices * capacity * block_rows, part_width), jnp.bfloat16
                        ),
                        pltpu.VMEM((devices * capacity * block_rows, own_rows), jnp.bfloat16),
                        pltpu.VMEM((rows, part_width), jnp.bfloat16),
                        pltpu.VMEM((4, GROUP * block_rows, own_rows), jnp.bfloat16),
                        pltpu.SemaphoreType.DMA,
                        pltpu.SemaphoreType.DMA((devices,)),
                        pltpu.SemaphoreType.DMA((4,)),
                    ],
                ),
                out_shape=jax.ShapeDtypeStruct((own_rows, part_width), jnp.float32),
                compiler_params=pltpu.CompilerParams(vmem_limit_bytes=VMEM_BYTES),
                cost_estimate=pl.CostEstimate(
                    flops=2 * requests * block_rows * own_rows * part_width,
                    bytes_accessed=slots * block_rows * own_rows * 2,
                    transcendentals=0,
                ),
                name="labels",
            )(
                step_tile, position, used, own_slot, own_place, me.reshape(1), weights, piece, factor,
                factor,
            )
        )
    return outs[0] if splits == 1 else jnp.concatenate(outs, axis=1)


def solution(mesh):
    in_specs = (P("dp", None), P("tensor"), P("dp", "tensor"), P("dp", None), P("dp"))
    out_specs = P("dp", "tensor")
    return jax.shard_map(
        on_device, mesh=mesh, in_specs=in_specs, out_specs=out_specs, check_vma=False
    )
```
